128 devices in a mesh: dp: 8 (over z_lo, x), tensor: 16 (over z_hi, y, core).
Axes of the slice: x: 4, y: 4, z: 4 (z_hi: 2, z_lo: 2; z = z_hi * 2 + z_lo), core: 2. Of those that a mesh axis runs over, the one named last changes fastest.
Arguments:
- tokens: bfloat16 [4096, 14784], P('dp', 'tensor'), may hold values from -6 to 6
- base_weight: bfloat16 [14784, 4096], P('tensor'), may hold values from -0.046875 to 0.046875
- first_factor: bfloat16 [32, 462, 128], P('tensor'), may hold values from -0.25 to 0.25
- second_factor: bfloat16 [32, 128, 128], P('tensor'), may hold values from -0.5 to 0.5
- channel_order: int32 [4096], replicated, may hold values from 0 to 4095, each once
- cotangent: bfloat16 [4096, 4096], P(('dp', 'tensor')), may hold values from -6 to 6
Outputs:
- output: float32 [4096, 4096], P(('dp', 'tensor'))
- d_tokens: float32 [4096, 14784], P('dp', 'tensor')
- d_first: float32 [32, 462, 128], P('tensor')
- d_second: float32 [32, 128, 128], P('tensor')
The draws below stay inside these ranges and needn't reach their ends.
Inputs may be any that keep to these rules, and one draw needn't show every extreme that they name: channel_order holds each of 0 to 4095 once.
All inputs are finite; a program needn't handle non-finite values.
Results may differ from the reference program's by a relative error of at most 0.0029.
Values may be sent and summed in bfloat16 or wider, within the bound.
No kernel may reach another device: no remote copies, remote signals or barrier semaphores. Data moves between devices by JAX's collectives and lax.ppermute only.
A program may use at most 128 MiB of HBM per device.

```python
import jax
import jax.numpy as jnp

NB = 32
BI = 462
BO = 128
FF = 14784
D = 4096
TOKENS = 4096


def block_scale(rng, dims, pieces, smallest, high):
    level = 1.0
    for dim, shards_of in pieces:
        heights = jax.random.uniform(jax.random.fold_in(jax.random.fold_in(rng, 6), dim), (shards_of,), jnp.float32, smallest / len(pieces), high / len(pieces))
        level = level * jnp.repeat(jnp.exp(heights), dims[dim] // shards_of).reshape((-1,) + (1,) * (len(dims) - 1 - dim))
    return level


def centred(key, shape, scale, bound, cuts=(), held_as=jnp.bfloat16):
    result = jax.random.normal(key, shape, jnp.float32) * scale
    if len(cuts) > 0:
        result = block_scale(key, shape, cuts, -0.22, 0.18) * result
    return jnp.clip(result, min=-bound, max=bound).astype(held_as)


def setup_inputs(seed: int = 0) -> dict:
    streams_of = jax.random.split(jax.random.key(seed), 7)
    return {
        "tokens": centred(streams_of[0], (TOKENS, FF), 1.0, 6.0, ((0, 8), (1, 16))),
        "base_weight": centred(streams_of[1], (FF, D), FF ** -0.5, 0.046875, ((0, 16),)),
        "first_factor": centred(streams_of[2], (NB, BI, BO), BI ** -0.5, 0.25, ((0, 16),)),
        "second_factor": centred(streams_of[3], (NB, BO, BO), BO ** -0.5, 0.5, ((0, 16),)),
        "channel_order": jax.random.permutation(streams_of[4], D).astype(jnp.int32),
        "cotangent": centred(streams_of[5], (TOKENS, D), 1.0, 6.0, ((0, 128),)),
    }


def block_apply(values, factor):
    return jnp.einsum("tnb,nbo->tno", values.astype(jnp.float32), factor.astype(jnp.float32))


def reference(tokens, base_weight, first_factor, second_factor, channel_order, cotangent):
    tok_total = tokens.shape[0]
    blocks_in = tokens.reshape(tok_total, NB, BI)
    base_out = jnp.dot(tokens, base_weight, preferred_element_type=jnp.float32)
    inner_act = block_apply(blocks_in, first_factor).reshape(tok_total, D).astype(jnp.bfloat16)
    mixed_in = jnp.take(inner_act, channel_order, axis=1)
    mixed_blocks = mixed_in.reshape(tok_total, NB, BO)
    delta_out = block_apply(mixed_blocks, second_factor).reshape(tok_total, D)
    output = base_out + delta_out
    grad_blocks = cotangent.reshape(tok_total, NB, BO).astype(jnp.float32)
    d_mixed = jnp.einsum("tno,nbo->tnb", grad_blocks, second_factor.astype(jnp.float32))
    d_mixed = d_mixed.reshape(tok_total, D).astype(jnp.bfloat16)
    d_second = jnp.einsum("tnb,tno->nbo", mixed_blocks.astype(jnp.float32), grad_blocks)
    inverse = jnp.argsort(channel_order).astype(jnp.int32)
    d_inner = jnp.take(d_mixed, inverse, axis=1)
    d_inner_blocks = d_inner.reshape(tok_total, NB, BO).astype(jnp.float32)
    d_first = jnp.einsum("tnb,tno->nbo", blocks_in.astype(jnp.float32), d_inner_blocks)
    d_base = jnp.dot(cotangent, base_weight.T, preferred_element_type=jnp.float32)
    d_delta = jnp.einsum("tno,nbo->tnb", d_inner_blocks, first_factor.astype(jnp.float32)).reshape(tok_total, FF)
    d_tokens = d_base + d_delta
    return (output, d_tokens, d_first, d_second)
```

```python
import jax
import jax.numpy as jnp
from jax import lax
from jax.sharding import Mesh, PartitionSpec as P

F32 = jnp.float32
BF16 = jnp.bfloat16
DP = ("zl", "x")
CHIPS = ("zh", "y")
TENSOR = ("zh", "y", "c")
OTHER_CORE = [(0, 1), (1, 0)]


def spread(value, axes, count):
    whole = jnp.broadcast_to(value[None], (count,) + value.shape)
    return lax.all_to_all(whole, axes, 0, 0)


def pair_up(mine, other, core):
    first = jnp.where(core == 0, mine, other)
    second = jnp.where(core == 0, other, mine)
    return jnp.stack([first, second], axis=1)


def per_device(tokens, base_weight, first_factor, second_factor, channel_order, cotangent):
    rows, hidden = tokens.shape
    blocks, block_in, block_out = first_factor.shape
    width = base_weight.shape[1]
    channels = blocks * block_out
    core = lax.axis_index("c")
    place = lax.axis_index(TENSOR)
    group = lax.axis_index(DP)
    chips = lax.axis_size(CHIPS)
    groups = lax.axis_size(DP)
    share = rows // (2 * chips)

    second_mine = spread(second_factor.reshape(channels, block_out), CHIPS, chips)
    cot_mine = spread(cotangent, CHIPS, chips)
    second_other = lax.ppermute(second_mine, "c", OTHER_CORE)
    second_all = pair_up(second_mine, second_other, core).reshape(-1, block_out, block_out)
    own = place * channels + jnp.arange(channels, dtype=jnp.int32)
    hits = (own[:, None] == channel_order[None, :]).astype(BF16).reshape(channels, -1, block_out)
    routed = jnp.einsum("knb,nbo->kno", hits, second_all, preferred_element_type=F32)
    routed = routed.reshape(channels, width).astype(BF16)

    wide = jnp.zeros((hidden, channels), BF16)
    for n in range(blocks):
        wide = wide.at[n * block_in : (n + 1) * block_in, n * block_out : (n + 1) * block_out].set(
            first_factor[n]
        )
    inner = jnp.dot(tokens, wide, preferred_element_type=F32).astype(BF16)

    def part(which):
        tok = lax.dynamic_index_in_dim(tokens.reshape(chips, 2, share, hidden), which, 1, False)
        inn = lax.dynamic_index_in_dim(inner.reshape(chips, 2, share, channels), which, 1, False)
        out = jnp.dot(tok.reshape(-1, hidden), base_weight, preferred_element_type=F32)
        return out + jnp.dot(inn.reshape(-1, channels), routed, preferred_element_type=F32)

    got = lax.ppermute(part(1 - core).astype(BF16), "c", OTHER_CORE)
    pair_sum = part(core) + got.astype(F32)
    terms = lax.all_to_all(pair_sum.astype(BF16).reshape(chips, share, width), CHIPS, 0, 0)
    output = jnp.sum(terms.astype(F32), axis=0)

    cot_other = lax.ppermute(cot_mine, "c", OTHER_CORE)
    cot_all = pair_up(cot_mine, cot_other, core).reshape(rows, width)
    d_inner = lax.dot_general(cot_all, routed, (((1,), (1,)), ((), ())), preferred_element_type=F32)
    d_inner = d_inner.astype(BF16)
    d_base = lax.dot_general(base_weight, cot_all, (((1,), (1,)), ((), ())), preferred_element_type=F32)
    d_delta = lax.dot_general(wide, d_inner, (((1,), (1,)), ((), ())), preferred_element_type=F32)
    d_tokens = (d_base + d_delta).T
    full = lax.dot_general(tokens, d_inner, (((0,), (0,)), ((), ())), preferred_element_type=F32)
    row = jnp.arange(hidden, dtype=jnp.int32)[:, None] // block_in
    d_first = full[:, :block_out]
    for n in range(1, blocks):
        d_first = jnp.where(row == n, full[:, n * block_out : (n + 1) * block_out], d_first)
    grads = lax.dot_general(inner, cot_all, (((0,), (0,)), ((), ())), preferred_element_type=F32)
    in_block = jnp.max(hits, axis=2).astype(F32)
    d_rows = jnp.sum(grads.reshape(channels, -1, block_out) * in_block[:, :, None], axis=1)

    first_share = -(-hidden // groups)
    row_share = channels // groups
    d_first = jnp.pad(d_first, ((0, first_share * groups - hidden), (0, 0)))
    sent = jnp.concatenate(
        [
            d_first.reshape(groups, first_share, block_out),
            d_rows.reshape(groups, row_share, block_out),
        ],
        axis=1,
    )
    sums = jnp.sum(lax.all_to_all(sent.astype(BF16), DP, 0, 0).astype(F32), axis=0)
    sums = sums.astype(BF16)
    rows_all = spread(sums[first_share:], TENSOR, 2 * chips).reshape(-1, block_out)
    wanted = lax.dynamic_slice_in_dim(channel_order, place * channels, channels, 0)
    held = (
        jnp.arange(2 * chips, dtype=jnp.int32)[:, None] * channels
        + group * row_share
        + jnp.arange(row_share, dtype=jnp.int32)[None, :]
    ).reshape(-1)
    pick = (wanted[:, None] == held[None, :]).astype(BF16)
    picked = jnp.dot(pick, rows_all, preferred_element_type=F32).astype(BF16)
    final = spread(jnp.concatenate([sums[:first_share], picked]), DP, groups)
    d_first = final[:, :first_share].reshape(-1, block_out)[:hidden].astype(F32)
    d_second = jnp.sum(final[:, first_share:].astype(F32), axis=0)
    return (
        output,
        d_tokens,
        d_first.reshape(blocks, block_in, block_out),
        d_second.reshape(blocks, block_out, block_out),
    )


def solution(mesh):
    fine = Mesh(mesh.devices.reshape(2, 4, 2, 4, 2), ("zl", "x", "zh", "y", "c"))
    return jax.shard_map(
        per_device,
        mesh=fine,
        in_specs=(
            P(DP, TENSOR),
            P(TENSOR, None),
            P(TENSOR, None, None),
            P(TENSOR, None, None),
            P(),
            P(DP + TENSOR, None),
        ),
        out_specs=(
            P(DP + TENSOR, None),
            P(DP, TENSOR),
            P(TENSOR, None, None),
            P(TENSOR, None, None),
        ),
        check_vma=False,
    )
```

```python
import jax
import jax.numpy as jnp
from jax import lax
from jax.experimental import pallas as pl
from jax.experimental.pallas import tpu as pltpu
from jax.sharding import Mesh, PartitionSpec as P

F32 = jnp.float32
BF16 = jnp.bfloat16
DP = ("zl", "x")
TENSOR = ("zh", "y", "c")
SWAP = [(0, 1), (1, 0)]
TURNS = (1, 3, 2)
VMEM = pl.BlockSpec(memory_space=pltpu.VMEM)
SMEM = pl.BlockSpec(memory_space=pltpu.SMEM)
ANY = pl.BlockSpec(memory_space=pl.ANY)
MIB = 1 << 20
CHUNKS = 10
HELD = ((0, 0, 0), (0, 1, 0), (1, 0, 1), (1, 1, 1), (2, 0, 3), (2, 1, 3), (3, 0, 2), (4, 0, 2))
SCALE = 100


def params(mib):
    return pltpu.CompilerParams(vmem_limit_bytes=mib * MIB)


def cost(flops, moved):
    return pl.CostEstimate(flops=flops // SCALE, bytes_accessed=moved // SCALE, transcendentals=0)


def turn(value, by):
    return lax.ppermute(value, "y", [(i, (i + by) % 4) for i in range(4)])


def spread(value, axes, count):
    whole = jnp.broadcast_to(value[None], (count,) + value.shape)
    return lax.all_to_all(whole, axes, 0, 0)


def dot(a, b):
    return jnp.dot(a, b, preferred_element_type=F32)


def dot_nt(a, b):
    return lax.dot_general(a, b, (((1,), (1,)), ((), ())), preferred_element_type=F32)


def base_rows(where, tokens, weight, other, own, held):
    step = pl.program_id(0)
    share = tokens.shape[0] // 16
    half = tokens.shape[0] // 2

    @pl.when(step == 0)
    def _():
        core, zh, y = where[0], where[1], where[2]
        for p in range(2):
            for z in range(2):
                for k in range(4):
                    c = 1 - core if p == 0 else core
                    zz = 1 - zh if z == 0 else zh
                    g = zz * 8 + lax.rem(y + (k + 1) % 4, 4) * 2 + c
                    at = p * half + (z * 4 + k) * share
                    held[at : at + share, :] = tokens[pl.ds(pl.multiple_of(g * share, share), share), :]

    total = dot(held[...], weight[...])
    other[...] = total[:half].astype(BF16)
    own[...] = total[half:]


def call_base_rows(where, tokens, weight, tile=1024):
    rows, hidden = tokens.shape
    width = weight.shape[1]
    half = rows // 2
    return pl.pallas_call(
        base_rows,
        grid=(width // tile,),
        in_specs=[
            SMEM,
            pl.BlockSpec((rows, hidden), lambda j: (0, 0)),
            pl.BlockSpec((hidden, tile), lambda j: (0, j)),
        ],
        out_specs=[pl.BlockSpec((half, tile), lambda j: (0, j))] * 2,
        out_shape=[
            jax.ShapeDtypeStruct((half, width), BF16),
            jax.ShapeDtypeStruct((half, width), F32),
        ],
        scratch_shapes=[pltpu.VMEM((rows, hidden), BF16)],
        compiler_params=params(60),
        name="base_rows",
        cost_estimate=cost(2 * rows * hidden * width, hidden * width * 2),
    )(where, tokens, weight)


def pair_sum(own, got, left, right, kept):
    total = own[...] + got[...].astype(F32)
    quarter = kept.shape[0]
    kept[...] = total[quarter:]
    step = pl.program_id(0)
    steps = pl.num_programs(0)

    @pl.when(step < steps // 2)
    def _():
        left[...] = total[:quarter].astype(BF16)

    @pl.when(step >= steps // 2)
    def _():
        right[...] = total[:quarter].astype(BF16)


def call_pair_sum(own, got, tile=1024):
    half, width = own.shape
    steps = width // tile
    mid = steps // 2
    out = (half // 2, tile)
    *sent, kept = pl.pallas_call(
        pair_sum,
        grid=(steps,),
        in_specs=[pl.BlockSpec((half, tile), lambda j: (0, j))] * 2,
        out_specs=[
            pl.BlockSpec(out, lambda j: (0, jnp.minimum(j, mid - 1))),
            pl.BlockSpec(out, lambda j: (0, jnp.maximum(j - mid, 0))),
            pl.BlockSpec(out, lambda j: (0, j)),
        ],
        out_shape=[jax.ShapeDtypeStruct((half // 2, width // 2), BF16)] * 2
        + [jax.ShapeDtypeStruct((half // 2, width), F32)],
        compiler_params=params(60),
        name="pair_sum",
        cost_estimate=cost(half * width, half * width * 9),
    )(own, got)
    return sent, kept


def quad_sum(kept, left, right, one, two, three, own):
    share = own.shape[0]
    first = pl.program_id(0) < pl.num_programs(0) // 2
    got = jnp.where(first, left[...], right[...]).astype(F32)
    for k, out in enumerate((one, two, three, own)):
        rows = slice(k * share, (k + 1) * share)
        out[...] = (kept[rows, :] + got[rows, :]).astype(out.dtype)


def call_quad_sum(kept, got, tile=1024):
    quarter, width = kept.shape
    share = quarter // 4
    steps = width // tile
    mid = steps // 2
    return pl.pallas_call(
        quad_sum,
        grid=(steps,),
        in_specs=[
            pl.BlockSpec((quarter, tile), lambda j: (0, j)),
            pl.BlockSpec((quarter, tile), lambda j: (0, jnp.minimum(j, mid - 1))),
            pl.BlockSpec((quarter, tile), lambda j: (0, jnp.maximum(j - mid, 0))),
        ],
        out_specs=[pl.BlockSpec((share, tile), lambda j: (0, j))] * 4,
        out_shape=[jax.ShapeDtypeStruct((share, width), BF16)] * 3
        + [jax.ShapeDtypeStruct((share, width), F32)],
        compiler_params=params(60),
        name="quad_sum",
        cost_estimate=cost(quarter * width, quarter * width * 8),
    )(kept, *got)


def reorder(order, inner, out, flat):
    count, share, channels = inner.shape
    block = order.shape[1]
    per = channels // block
    tiles = count * per
    for t in range(tiles):
        flat[t] = inner[t // per, :, (t % per) * block : (t % per + 1) * block].astype(F32)

    def one(j, _):
        wanted = jnp.broadcast_to(order[pl.ds(j, 1), :], (share, block))
        lane = wanted % block
        tile = wanted // block
        total = jnp.zeros((share, block), F32)
        for t in range(tiles):
            found = jnp.take_along_axis(flat[t], lane, axis=1, mode="promise_in_bounds")
            total = jnp.where(tile == t, found, total)
        out[j] = total.astype(BF16)
        return 0

    lax.fori_loop(0, tiles, one, 0)


def call_reorder(order, inner):
    count, share, channels = inner.shape
    tiles, block = order.shape
    return pl.pallas_call(
        reorder,
        in_specs=[VMEM] * 2,
        out_specs=VMEM,
        out_shape=jax.ShapeDtypeStruct((tiles, share, block), BF16),
        scratch_shapes=[pltpu.VMEM((tiles, share, block), F32)],
        compiler_params=params(60),
        name="reorder",
        cost_estimate=cost(tiles * tiles * share * block * 4, count * share * channels * 4),
    )(order, inner)


def sources(where):
    core, zh, y = where[0], where[1], where[2]
    found = []
    for c in range(2):
        for slot, (chunk, row, back) in enumerate(HELD):
            cc = core if c == 0 else 1 - core
            zz = zh if slot % 2 == 0 else 1 - zh
            place = zz * 8 + lax.rem(y + 4 - back, 4) * 2 + cc
            found.append((c * 5 + chunk, row, place))
    return found


def block_of(ref, z, i, share, block, base=0):
    each = block // share
    parts = [
        ref[z * share : (z + 1) * share, base + (i * each + q) * block : base + (i * each + q + 1) * block]
        for q in range(each)
    ]
    return jnp.concatenate(parts, axis=0)


def last_sum(where, own, one, two, three, mixed, *refs):
    chunks, out = refs[:CHUNKS], refs[CHUNKS]
    share = own.shape[0]
    block = mixed.shape[2]
    for chunk, z, g in sources(where):
        for i in range(2):
            n = g * 2 + i
            cols = pl.ds(pl.multiple_of(n * block, block), block)
            delta = dot(mixed[n], block_of(chunks[chunk], z, i, share, block))
            out[:, cols] = (
                delta
                + own[:, cols]
                + one[:, cols].astype(F32)
                + two[:, cols].astype(F32)
                + three[:, cols].astype(F32)
            )


def call_last_sum(where, own, parts, mixed, chunks):
    share, width = own.shape
    tiles, _, block = mixed.shape
    per = chunks[0].shape[1] - width
    second = [pl.BlockSpec((v.shape[0], per), lambda j: (0, width // per)) for v in chunks]
    whole = pl.BlockSpec((share, width), lambda j: (0, 0))
    return pl.pallas_call(
        last_sum,
        grid=(1,),
        in_specs=[SMEM] + [whole] * 4 + [pl.BlockSpec(mixed.shape, lambda j: (0, 0, 0))] + second,
        out_specs=whole,
        out_shape=jax.ShapeDtypeStruct((share, width), F32),
        compiler_params=params(60),
        name="last_sum",
        cost_estimate=cost(2 * share * width * block, share * width * 16),
    )(where, own, *parts, mixed, *chunks)


def factor_grads(where, order, mixed, tokens_t, *refs):
    chunks, (d_inner, sums, cot, routed) = refs[:CHUNKS], refs[CHUNKS:]
    core, zh, y = where[0], where[1], where[2]
    block = order.shape[1]
    rows, channels = d_inner.shape
    share = rows // 16
    width = cot.shape[1]
    hidden = tokens_t.shape[0]
    found = sources(where)
    place = zh * 8 + y * 2 + core
    row = lax.broadcasted_iota(jnp.int32, (channels, block), 0) + place * channels
    for chunk, z, g in found:
        cot[pl.ds(pl.multiple_of(g * share, share), share), :] = chunks[chunk][
            z * share : (z + 1) * share, :width
        ]
        for i in range(2):
            n = g * 2 + i
            hits = jnp.where(row == order[pl.ds(n, 1), :], 1.0, 0.0).astype(BF16)
            factor = block_of(chunks[chunk], z, i, share, block, width)
            cols = pl.ds(pl.multiple_of(n * block, block), block)
            routed[:, cols] = dot(hits, factor).astype(BF16)
    grad = dot_nt(cot[...], routed[...]).astype(BF16)
    d_inner[...] = grad
    whole = dot(tokens_t[...], grad)
    unit = lax.broadcasted_iota(jnp.int32, (hidden, block), 0)
    d_first = jnp.where(unit < hidden // 2, whole[:, :block], whole[:, block:]).astype(BF16)
    each = sums.shape[0] // 8
    few = channels // 8
    room = each - few
    for k in range(8):
        have = min(room, hidden - k * room)
        if have < room:
            sums[k * each : k * each + room, :] = jnp.zeros((room, block), BF16)
        sums[k * each : k * each + have, :] = d_first[k * room : k * room + have]
    mixed_t = mixed[...].reshape(rows, channels).T
    for i in range(channels // block):
        n = place * 2 + i
        cols = pl.ds(pl.multiple_of(n * block, block), block)
        d_second = dot(mixed_t[i * block : (i + 1) * block, :], cot[:, cols]).astype(BF16)
        for q in range(block // few):
            k = i * (block // few) + q
            sums[k * each + room : (k + 1) * each, :] = d_second[q * few : (q + 1) * few]


def call_factor_grads(where, order, mixed, tokens_t, chunks, room):
    groups, share, channels = mixed.shape
    rows = groups * share
    tiles, block = order.shape
    width = tiles * block
    each = room + channels // 8
    return pl.pallas_call(
        factor_grads,
        in_specs=[SMEM] + [VMEM] * (3 + CHUNKS),
        out_specs=[VMEM] * 2,
        out_shape=[
            jax.ShapeDtypeStruct((rows, channels), BF16),
            jax.ShapeDtypeStruct((8 * each, block), BF16),
        ],
        scratch_shapes=[pltpu.VMEM((rows, width), BF16), pltpu.VMEM((channels, width), BF16)],
        compiler_params=params(60),
        name="factor_grads",
        cost_estimate=cost(4 * rows * channels * width, rows * width * 2),
    )(where, order, mixed, tokens_t, *chunks)


def token_grads(where, weight, wide, d_inner, *refs):
    chunks, (out, cot) = refs[:CHUNKS], refs[CHUNKS:]
    share = cot.shape[0] // 16
    for chunk, z, g in sources(where):
        cot[pl.ds(pl.multiple_of(g * share, share), share), :] = chunks[chunk][
            z * share : (z + 1) * share, :
        ]
    term = dot_nt(weight[...], cot[...])

    @pl.when(pl.program_id(0) == 0)
    def _():
        out[...] = term + dot_nt(wide[...], d_inner[...])

    @pl.when(pl.program_id(0) > 0)
    def _():
        out[...] += term


def call_token_grads(where, weight, wide, d_inner, chunks, tile=1024):
    hidden, width = weight.shape
    rows, channels = d_inner.shape
    return pl.pallas_call(
        token_grads,
        grid=(width // tile,),
        in_specs=[
            SMEM,
            pl.BlockSpec((hidden, tile), lambda k: (0, k)),
            pl.BlockSpec((hidden, channels), lambda k: (0, 0)),
            pl.BlockSpec((rows, channels), lambda k: (0, 0)),
        ]
        + [pl.BlockSpec((v.shape[0], tile), lambda k: (0, k)) for v in chunks],
        out_specs=pl.BlockSpec((hidden, rows), lambda k: (0, 0)),
        out_shape=jax.ShapeDtypeStruct((hidden, rows), F32),
        scratch_shapes=[pltpu.VMEM((rows, tile), BF16)],
        compiler_params=params(60),
        name="token_grads",
        cost_estimate=cost(2 * rows * hidden * width, hidden * width * 2),
    )(where, weight, wide, d_inner, *chunks)


def per_device(tokens, base_weight, first_factor, second_factor, channel_order, cotangent):
    rows, hidden = tokens.shape
    blocks, block_in, block_out = first_factor.shape
    width = base_weight.shape[1]
    channels = blocks * block_out
    share = rows // 16
    room = -(-hidden // 128) * 16
    hold = lax.optimization_barrier
    where = jnp.stack([lax.axis_index("c"), lax.axis_index("zh"), lax.axis_index("y")])
    where = where.astype(jnp.int32)
    order = channel_order.reshape(-1, block_out)

    packed = second_factor.reshape(-1, share, block_out).transpose(1, 0, 2).reshape(share, -1)
    bundle = jnp.concatenate([cotangent, packed], axis=1)
    partner = lax.ppermute(bundle, "zh", SWAP)
    wide = jnp.concatenate(
        [
            jnp.pad(first_factor[n], ((0, 0), (n * block_out, channels - (n + 1) * block_out)))
            for n in range(blocks)
        ]
    )
    inner = dot(tokens, wide).astype(BF16).reshape(16, share, channels)
    bundle, partner, wide, inner, tokens = hold((bundle, partner, wide, inner, tokens))

    pair = jnp.concatenate([bundle, partner], axis=0)
    next_y, last_y = turn(pair, 1), turn(pair, 3)
    inner = lax.all_to_all(inner, TENSOR, 0, 0)
    other, own = call_base_rows(where, tokens, base_weight)
    pair, next_y, last_y, inner, other, own = hold((pair, next_y, last_y, inner, other, own))

    got = lax.ppermute(other, "c", SWAP)
    far = turn(pair[:share], 2)
    mine = [pair, next_y, last_y]
    theirs = [lax.ppermute(v, "c", SWAP) for v in mine]
    mixed = call_reorder(order, inner)
    sent, kept = call_pair_sum(own, got)
    far, theirs, mixed, sent, kept, pair = hold((far, theirs, mixed, sent, kept, pair))

    left = lax.ppermute(sent[0], "zh", SWAP)
    far_z = turn(pair[share:], 2)
    mixed_mine = mixed.reshape(16, blocks, share, block_out).transpose(0, 2, 1, 3)
    mixed_mine = lax.all_to_all(mixed_mine.reshape(16, share, channels), TENSOR, 0, 0)
    left, far, far_z, mixed_mine, right = hold((left, far, far_z, mixed_mine, sent[1]))

    right = lax.ppermute(right, "zh", SWAP)
    theirs = theirs + [lax.ppermute(v, "c", SWAP) for v in (far, far_z)]
    chunks = mine + [far, far_z] + theirs
    d_inner, sums = call_factor_grads(where, order, mixed_mine, tokens.T, chunks, room)
    sums = lax.all_to_all(sums.reshape(8, -1, block_out), DP, 0, 0)
    right, sums, d_inner = hold((right, sums, d_inner))

    terms = call_quad_sum(kept, [left, right])
    parts = [turn(terms[d - 1], d) for d in (1, 2, 3)]
    sums = jnp.sum(sums.astype(F32), axis=0).astype(BF16)
    final = spread(sums, DP, 8)
    d_tokens = call_token_grads(where, base_weight, wide, d_inner, chunks).T
    parts, final, d_tokens = hold((parts, final, d_tokens))

    output = call_last_sum(where, terms[3], parts, mixed, chunks)
    d_first = final[:, :room].reshape(-1, block_out)[:hidden].astype(F32)
    d_second = final[:, room:].astype(F32)
    return (
        output,
        d_tokens,
        d_first.reshape(blocks, block_in, block_out),
        d_second.reshape(blocks, block_out, block_out),
    )


def solution(mesh):
    fine = Mesh(mesh.devices.reshape(2, 4, 2, 4, 2), ("zl", "x", "zh", "y", "c"))
    return jax.shard_map(
        per_device,
        mesh=fine,
        in_specs=(
            P(DP, TENSOR),
            P(TENSOR, None),
            P(TENSOR, None, None),
            P(TENSOR, None, None),
            P(),
            P(DP + TENSOR, None),
        ),
        out_specs=(
            P(DP + TENSOR, None),
            P(DP, TENSOR),
            P(TENSOR, None, None),
            P(TENSOR, None, None),
        ),
        check_vma=False,
    )
```

```python
import jax
import jax.numpy as jnp
from jax import lax
from jax.experimental import pallas as pl
from jax.experimental.pallas import tpu as pltpu
from jax.sharding import Mesh, PartitionSpec as P

F32 = jnp.float32
BF16 = jnp.bfloat16
DP = ("zl", "x")
TENSOR = ("zh", "y", "c")
SWAP = [(0, 1), (1, 0)]
TURNS = (1, 3, 2)
VMEM = pl.BlockSpec(memory_space=pltpu.VMEM)
ANY = pl.BlockSpec(memory_space=pl.ANY)
MIB = 1 << 20
CHUNKS = 10
HELD = ((0, 0, 0), (0, 1, 0), (1, 0, 1), (1, 1, 1), (2, 0, 3), (2, 1, 3), (3, 0, 2), (4, 0, 2))
SCALE = 100
KEPT = BF16
LEFT = 1
TILE = 2048


def params(mib):
    return pltpu.CompilerParams(vmem_limit_bytes=mib * MIB)


def cost(flops, moved):
    return pl.CostEstimate(flops=flops // SCALE, bytes_accessed=moved // SCALE, transcendentals=0)


def turn(value, by):
    return lax.ppermute(value, "y", [(i, (i + by) % 4) for i in range(4)])


def spread(value, axes, count):
    whole = jnp.broadcast_to(value[None], (count,) + value.shape)
    return lax.all_to_all(whole, axes, 0, 0)


def place_of():
    return lax.axis_index("c"), lax.axis_index("zh"), lax.axis_index("y")


def dot(a, b):
    return jnp.dot(a, b, preferred_element_type=F32)


def dot_nt(a, b):
    return lax.dot_general(a, b, (((1,), (1,)), ((), ())), preferred_element_type=F32)


def pack(cotangent, second, out):
    share, width = cotangent.shape
    block = second.shape[1]
    out[:, :width] = cotangent[...]
    for q in range(second.shape[0] // share):
        out[:, width + q * block : width + (q + 1) * block] = second[q * share : (q + 1) * share, :]


def call_pack(cotangent, second):
    share, width = cotangent.shape
    return pl.pallas_call(
        pack,
        in_specs=[VMEM] * 2,
        out_specs=VMEM,
        out_shape=jax.ShapeDtypeStruct((share, width + second.size // share), BF16),
        compiler_params=params(60),
        name="pack",
        cost_estimate=cost(share, share * width * 4),
    )(cotangent, second)


def base_rows(tokens, weight, other, own, held):
    step = pl.program_id(0)
    share = tokens.shape[0] // 16
    half = tokens.shape[0] // 2

    @pl.when(step == 0)
    def _():
        core, zh, y = place_of()
        for p in range(2):
            for z in range(2):
                for k in range(4):
                    c = 1 - core if p == 0 else core
                    zz = 1 - zh if z == 0 else zh
                    g = zz * 8 + lax.rem(y + (k + 1) % 4, 4) * 2 + c
                    at = p * half + (z * 4 + k) * share
                    held[at : at + share, :] = tokens[pl.ds(pl.multiple_of(g * share, share), share), :]

    total = dot(held[...], weight[...])
    other[...] = total[:half].astype(BF16)
    own[...] = total[half:].astype(own.dtype)


def call_base_rows(tokens, weight, tile=1024):
    rows, hidden = tokens.shape
    width = weight.shape[1]
    half = rows // 2
    return pl.pallas_call(
        base_rows,
        grid=(width // tile,),
        in_specs=[
            pl.BlockSpec((rows, hidden), lambda j: (0, 0)),
            pl.BlockSpec((hidden, tile), lambda j: (0, j)),
        ],
        out_specs=[pl.BlockSpec((half, tile), lambda j: (0, j))] * 2,
        out_shape=[
            jax.ShapeDtypeStruct((half, width), BF16),
            jax.ShapeDtypeStruct((half, width), KEPT),
        ],
        scratch_shapes=[pltpu.VMEM((rows, hidden), BF16)],
        compiler_params=params(60),
        name="base_rows",
        cost_estimate=cost(2 * rows * hidden * width, hidden * width * 2),
    )(tokens, weight)


def pair_sum(own, got, left, right, kept):
    total = own[...].astype(F32) + got[...].astype(F32)
    quarter = kept.shape[0]
    kept[...] = total[quarter:].astype(kept.dtype)
    step = pl.program_id(0)

    @pl.when(step < LEFT)
    def _():
        left[...] = total[:quarter].astype(BF16)

    @pl.when(step >= LEFT)
    def _():
        right[...] = total[:quarter].astype(BF16)


def call_pair_sum(own, got, tile=1024):
    half, width = own.shape
    steps = width // tile
    out = (half // 2, tile)
    *sent, kept = pl.pallas_call(
        pair_sum,
        grid=(steps,),
        in_specs=[pl.BlockSpec((half, tile), lambda j: (0, j))] * 2,
        out_specs=[
            pl.BlockSpec(out, lambda j: (0, jnp.minimum(j, LEFT - 1))),
            pl.BlockSpec(out, lambda j: (0, jnp.maximum(j - LEFT, 0))),
            pl.BlockSpec(out, lambda j: (0, j)),
        ],
        out_shape=[
            jax.ShapeDtypeStruct((half // 2, LEFT * tile), BF16),
            jax.ShapeDtypeStruct((half // 2, width - LEFT * tile), BF16),
            jax.ShapeDtypeStruct((half // 2, width), KEPT),
        ],
        compiler_params=params(12),
        name="pair_sum",
        cost_estimate=cost(half * width, half * width * 6),
    )(own, got)
    return sent, kept


def quad_sum(kept, left, right, one, two, three, own):
    share = own.shape[0]
    cut = left.shape[1]
    for k, out in enumerate((one, two, three, own)):
        rows = slice(k * share, (k + 1) * share)
        out[:, :cut] = (kept[rows, :cut].astype(F32) + left[rows, :].astype(F32)).astype(out.dtype)
        out[:, cut:] = (kept[rows, cut:].astype(F32) + right[rows, :].astype(F32)).astype(out.dtype)


def call_quad_sum(kept, got):
    quarter, width = kept.shape
    share = quarter // 4
    return pl.pallas_call(
        quad_sum,
        in_specs=[VMEM] * 3,
        out_specs=[VMEM] * 4,
        out_shape=[jax.ShapeDtypeStruct((share, width), BF16)] * 3
        + [jax.ShapeDtypeStruct((share, width), F32)],
        compiler_params=params(60),
        name="quad_sum",
        cost_estimate=cost(quarter * width, quarter * width * 8),
    )(kept, *got)


def reorder(order, inner, out, flat):
    count, share, channels = inner.shape
    block = order.shape[1]
    per = channels // block
    tiles = count * per
    for t in range(tiles):
        flat[t] = inner[t // per, :, (t % per) * block : (t % per + 1) * block].astype(F32)

    def one(j):
        wanted = jnp.broadcast_to(order[pl.ds(j, 1), :], (share, block))
        lane = wanted % block
        tile = wanted // block
        total = jnp.zeros((share, block), F32)
        for t in range(tiles):
            found = jnp.take_along_axis(flat[t], lane, axis=1, mode="promise_in_bounds")
            total = jnp.where(tile == t, found, total)
        return total.astype(BF16)

    def group(g, _):
        for i in range(per):
            out[g, :, i * block : (i + 1) * block] = one(g * per + i)
        return 0

    lax.fori_loop(0, count, group, 0)


def call_reorder(order, inner):
    count, share, channels = inner.shape
    tiles, block = order.shape
    return pl.pallas_call(
        reorder,
        in_specs=[VMEM] * 2,
        out_specs=VMEM,
        out_shape=jax.ShapeDtypeStruct(inner.shape, BF16),
        scratch_shapes=[pltpu.VMEM((tiles, share, block), F32)],
        compiler_params=params(6),
        name="reorder",
        cost_estimate=cost(tiles * tiles * share * block * 4, count * share * channels * 4),
    )(order, inner)


def sources():
    core, zh, y = place_of()
    found = []
    for c in range(2):
        for slot, (chunk, row, back) in enumerate(HELD):
            cc = core if c == 0 else 1 - core
            zz = zh if slot % 2 == 0 else 1 - zh
            place = zz * 8 + lax.rem(y + 4 - back, 4) * 2 + cc
            found.append((c * 5 + chunk, row, place))
    return found


def block_of(ref, z, i, share, block, base=0):
    each = block // share
    parts = [
        ref[z * share : (z + 1) * share, base + (i * each + q) * block : base + (i * each + q + 1) * block]
        for q in range(each)
    ]
    return jnp.concatenate(parts, axis=0)


def delta_rows(mixed, *refs):
    chunks, out = refs[:CHUNKS], refs[CHUNKS]
    share = out.shape[0]
    block = mixed.shape[2] // 2
    for chunk, z, g in sources():
        for i in range(2):
            cols = pl.ds(pl.multiple_of((g * 2 + i) * block, block), block)
            factor = block_of(chunks[chunk], z, i, share, block)
            out[:, cols] = dot(mixed[g, :, i * block : (i + 1) * block], factor)


def call_delta_rows(mixed, chunks):
    groups, share, channels = mixed.shape
    width = groups * channels
    per = chunks[0].shape[1] - width
    second = [pl.BlockSpec((v.shape[0], per), lambda j: (0, width // per)) for v in chunks]
    return pl.pallas_call(
        delta_rows,
        grid=(1,),
        in_specs=[pl.BlockSpec(mixed.shape, lambda j: (0, 0, 0))] + second,
        out_specs=pl.BlockSpec((share, width), lambda j: (0, 0)),
        out_shape=jax.ShapeDtypeStruct((share, width), F32),
        compiler_params=params(60),
        name="delta_rows",
        cost_estimate=cost(share * width * channels, share * width * 6),
    )(mixed, *chunks)


def factor_grads(order, mixed, tokens_t, *refs):
    chunks, (d_inner, sums, cot_out, cot, routed, sem) = refs[:CHUNKS], refs[CHUNKS:]
    core, zh, y = place_of()
    block = order.shape[1]
    rows, channels = d_inner.shape
    share = rows // 16
    width = cot.shape[1]
    hidden = tokens_t.shape[0]
    found = sources()
    place = zh * 8 + y * 2 + core
    row = lax.broadcasted_iota(jnp.int32, (channels, block), 0) + place * channels
    for chunk, z, g in found:
        cot[pl.ds(pl.multiple_of(g * share, share), share), :] = chunks[chunk][
            z * share : (z + 1) * share, :width
        ]
        for i in range(2):
            n = g * 2 + i
            hits = jnp.where(row == order[pl.ds(n, 1), :], 1.0, 0.0).astype(BF16)
            factor = block_of(chunks[chunk], z, i, share, block, width)
            cols = pl.ds(pl.multiple_of(n * block, block), block)
            routed[:, cols] = dot(hits, factor).astype(BF16)
    copy = pltpu.make_async_copy(cot, cot_out, sem)
    copy.start()
    grad = dot_nt(cot[...], routed[...]).astype(BF16)
    d_inner[...] = grad
    whole = dot(tokens_t[...], grad)
    unit = lax.broadcasted_iota(jnp.int32, (hidden, block), 0)
    d_first = jnp.where(unit < hidden // 2, whole[:, :block], whole[:, block:]).astype(BF16)
    each = sums.shape[0] // 8
    few = channels // 8
    room = each - few
    for k in range(8):
        have = min(room, hidden - k * room)
        if have < room:
            sums[k * each : k * each + room, :] = jnp.zeros((room, block), BF16)
        sums[k * each : k * each + have, :] = d_first[k * room : k * room + have]
    mixed_t = mixed[...].reshape(rows, channels).T
    for i in range(channels // block):
        n = place * 2 + i
        cols = pl.ds(pl.multiple_of(n * block, block), block)
        d_second = dot(mixed_t[i * block : (i + 1) * block, :], cot[:, cols]).astype(BF16)
        for q in range(block // few):
            k = i * (block // few) + q
            sums[k * each + room : (k + 1) * each, :] = d_second[q * few : (q + 1) * few]
    copy.wait()


def call_factor_grads(order, mixed, tokens_t, chunks, room):
    groups, share, channels = mixed.shape
    rows = groups * share
    tiles, block = order.shape
    width = tiles * block
    each = room + channels // 8
    return pl.pallas_call(
        factor_grads,
        in_specs=[VMEM] * (3 + CHUNKS),
        out_specs=[VMEM, VMEM, ANY],
        out_shape=[
            jax.ShapeDtypeStruct((rows, channels), BF16),
            jax.ShapeDtypeStruct((8 * each, block), BF16),
            jax.ShapeDtypeStruct((rows, width), BF16),
        ],
        scratch_shapes=[
            pltpu.VMEM((rows, width), BF16),
            pltpu.VMEM((channels, width), BF16),
            pltpu.SemaphoreType.DMA,
        ],
        compiler_params=params(60),
        name="factor_grads",
        cost_estimate=cost(4 * rows * channels * width, rows * width * 2),
    )(order, mixed, tokens_t, *chunks)


def token_grads(weight, cot, factor, d_inner, out, weight_held, cot_held, weight_sems, cot_sems):
    steps = weight_sems.shape[0]
    tile = weight.shape[1] // steps
    cols = [slice(k * tile, (k + 1) * tile) for k in range(steps)]
    copies = []
    for k, c in enumerate(cols):
        copies.append(pltpu.make_async_copy(cot.at[:, c], cot_held.at[:, c], cot_sems.at[k]))
        copies.append(pltpu.make_async_copy(weight.at[:, c], weight_held.at[:, c], weight_sems.at[k]))
    for copy in copies:
        copy.start()
    hidden, block = factor.shape
    unit = lax.broadcasted_iota(jnp.int32, (hidden, block), 0)
    zero = jnp.zeros((hidden, block), BF16)
    first = jnp.where(unit < hidden // 2, factor[...], zero)
    second = jnp.where(unit < hidden // 2, zero, factor[...])
    out[...] = dot_nt(jnp.concatenate([first, second], axis=1), d_inner[...])
    for k, c in enumerate(cols):
        copies[2 * k].wait()
        copies[2 * k + 1].wait()
        out[...] += dot_nt(weight_held[:, c], cot_held[:, c])


def call_token_grads(weight, cot, factor, d_inner, tile=1024):
    hidden, width = weight.shape
    rows, channels = d_inner.shape
    return pl.pallas_call(
        token_grads,
        in_specs=[ANY, ANY, VMEM, VMEM],
        out_specs=VMEM,
        out_shape=jax.ShapeDtypeStruct((hidden, rows), F32),
        scratch_shapes=[
            pltpu.VMEM((hidden, width), BF16),
            pltpu.VMEM((rows, width), BF16),
            pltpu.SemaphoreType.DMA((width // tile,)),
            pltpu.SemaphoreType.DMA((width // tile,)),
        ],
        compiler_params=params(60),
        name="token_grads",
        cost_estimate=cost(2 * rows * hidden * width, hidden * width * 2),
    )(weight, cot, factor, d_inner)


def per_device(tokens, base_weight, first_factor, second_factor, channel_order, cotangent):
    rows, hidden = tokens.shape
    blocks, block_in, block_out = first_factor.shape
    width = base_weight.shape[1]
    channels = blocks * block_out
    share = rows // 16
    room = -(-hidden // 128) * 16
    hold = lax.optimization_barrier
    order = channel_order.reshape(-1, block_out)

    bundle = call_pack(cotangent, second_factor.reshape(channels, block_out))
    partner = lax.ppermute(bundle, "zh", SWAP)
    factor = first_factor.reshape(hidden, block_out)
    block = jnp.arange(hidden, dtype=jnp.int32)[:, None] // block_in
    wide = jnp.concatenate([jnp.where(block == n, factor, 0) for n in range(blocks)], axis=1)
    inner = dot(tokens, wide).astype(BF16).reshape(16, share, channels)
    inner = lax.all_to_all(inner, TENSOR, 0, 0)
    other, own = call_base_rows(tokens, base_weight)
    bundle, partner, factor, inner, other, own = hold((bundle, partner, factor, inner, other, own))

    pair = jnp.concatenate([bundle, partner], axis=0)
    next_y, last_y = turn(pair, 1), turn(pair, 3)
    mixed = call_reorder(order, inner)
    sent, kept = call_pair_sum(own, lax.ppermute(other, "c", SWAP))
    left = lax.ppermute(sent[0], "zh", SWAP)
    theirs = [lax.ppermute(pair, "c", SWAP)]
    pair, next_y, last_y, mixed, left, right, kept, theirs = hold(
        (pair, next_y, last_y, mixed, left, sent[1], kept, theirs)
    )

    far = [turn(next_y[:share], 1), turn(last_y[share:], 3)]
    mine = [pair, next_y, last_y]
    theirs = theirs + [lax.ppermute(v, "c", SWAP) for v in mine[1:]]
    right = lax.ppermute(right, "zh", SWAP)
    mixed_mine = lax.all_to_all(mixed, TENSOR, 0, 0)
    far, theirs, left, right, mixed_mine = hold((far, theirs, left, right, mixed_mine))

    chunks = mine + far + theirs + [lax.ppermute(v, "c", SWAP) for v in far]
    d_inner, sums, cot = call_factor_grads(order, mixed_mine, tokens.T, chunks, room)
    sums = lax.all_to_all(sums.reshape(8, -1, block_out), DP, 0, 0)
    terms = call_quad_sum(kept, [left, right])
    delta = call_delta_rows(mixed, chunks)
    terms, sums, cot, delta = hold((terms, sums, cot, delta))

    parts = [turn(terms[d - 1], d) for d in (1, 2, 3)]
    sums = jnp.sum(sums.astype(F32), axis=0).astype(BF16)
    final = spread(sums, DP, 8)
    d_tokens = call_token_grads(base_weight, cot, factor, d_inner).T
    parts, d_tokens = hold((parts, d_tokens))

    output = terms[3] + delta
    for part in parts:
        output = output + part.astype(F32)
    d_first = final[:, :room].reshape(-1, block_out)[:hidden].astype(F32)
    d_second = final[:, room:].astype(F32)
    return (
        output,
        d_tokens,
        d_first.reshape(blocks, block_in, block_out),
        d_second.reshape(blocks, block_out, block_out),
    )


def solution(mesh):
    fine = Mesh(mesh.devices.reshape(2, 4, 2, 4, 2), ("zl", "x", "zh", "y", "c"))
    return jax.shard_map(
        per_device,
        mesh=fine,
        in_specs=(
            P(DP, TENSOR),
            P(TENSOR, None),
            P(TENSOR, None, None),
            P(TENSOR, None, None),
            P(),
            P(DP + TENSOR, None),
        ),
        out_specs=(
            P(DP + TENSOR, None),
            P(DP, TENSOR),
            P(TENSOR, None, None),
            P(TENSOR, None, None),
        ),
        check_vma=False,
    )
```

```python
import jax
import jax.numpy as jnp
from jax import lax
from jax.experimental import pallas as pl
from jax.experimental.pallas import tpu as pltpu
from jax.sharding import Mesh, PartitionSpec as P

F32 = jnp.float32
BF16 = jnp.bfloat16
DP = ("zl", "x")
TENSOR = ("zh", "y", "c")
SWAP = [(0, 1), (1, 0)]
TURNS = (1, 3, 2)
VMEM = pl.BlockSpec(memory_space=pltpu.VMEM)
ANY = pl.BlockSpec(memory_space=pl.ANY)
MIB = 1 << 20
CHUNKS = 10
HELD = ((0, 0, 0), (0, 1, 0), (1, 0, 1), (1, 1, 1), (2, 0, 3), (2, 1, 3), (3, 0, 2), (4, 0, 2))
SCALE = 100
KEPT = BF16
LEFT = 1
TILE = 2048


def params(mib):
    return pltpu.CompilerParams(vmem_limit_bytes=mib * MIB)


def cost(flops, moved):
    return pl.CostEstimate(flops=flops // SCALE, bytes_accessed=moved // SCALE, transcendentals=0)


def turn(value, by):
    return lax.ppermute(value, "y", [(i, (i + by) % 4) for i in range(4)])


def spread(value, axes, count):
    whole = jnp.broadcast_to(value[None], (count,) + value.shape)
    return lax.all_to_all(whole, axes, 0, 0)


def place_of():
    return lax.axis_index("c"), lax.axis_index("zh"), lax.axis_index("y")


def dot(a, b):
    return jnp.dot(a, b, preferred_element_type=F32)


def dot_nt(a, b):
    return lax.dot_general(a, b, (((1,), (1,)), ((), ())), preferred_element_type=F32)


def pack(cotangent, second, out):
    share, width = cotangent.shape
    block = second.shape[1]
    out[:, :width] = cotangent[...]
    for q in range(second.shape[0] // share):
        out[:, width + q * block : width + (q + 1) * block] = second[q * share : (q + 1) * share, :]


def call_pack(cotangent, second):
    share, width = cotangent.shape
    return pl.pallas_call(
        pack,
        in_specs=[VMEM] * 2,
        out_specs=VMEM,
        out_shape=jax.ShapeDtypeStruct((share, width + second.size // share), BF16),
        compiler_params=params(60),
        name="pack",
        cost_estimate=cost(share, share * width * 4),
    )(cotangent, second)


def base_rows(tokens, weight, other, own, held):
    step = pl.program_id(0)
    share = tokens.shape[0] // 16
    half = tokens.shape[0] // 2

    @pl.when(step == 0)
    def _():
        core, zh, y = place_of()
        for p in range(2):
            for z in range(2):
                for k in range(4):
                    c = 1 - core if p == 0 else core
                    zz = 1 - zh if z == 0 else zh
                    g = zz * 8 + lax.rem(y + (k + 1) % 4, 4) * 2 + c
                    at = p * half + (z * 4 + k) * share
                    held[at : at + share, :] = tokens[pl.ds(pl.multiple_of(g * share, share), share), :]

    total = dot(held[...], weight[...])
    other[...] = total[:half].astype(BF16)
    own[...] = total[half:].astype(own.dtype)


def call_base_rows(tokens, weight, tile=1024):
    rows, hidden = tokens.shape
    width = weight.shape[1]
    half = rows // 2
    return pl.pallas_call(
        base_rows,
        grid=(width // tile,),
        in_specs=[
            pl.BlockSpec((rows, hidden), lambda j: (0, 0)),
            pl.BlockSpec((hidden, tile), lambda j: (0, j)),
        ],
        out_specs=[pl.BlockSpec((half, tile), lambda j: (0, j))] * 2,
        out_shape=[
            jax.ShapeDtypeStruct((half, width), BF16),
            jax.ShapeDtypeStruct((half, width), KEPT),
        ],
        scratch_shapes=[pltpu.VMEM((rows, hidden), BF16)],
        compiler_params=params(60),
        name="base_rows",
        cost_estimate=cost(2 * rows * hidden * width, hidden * width * 2),
    )(tokens, weight)


def pair_sum(own, got, left, right, kept):
    total = own[...].astype(F32) + got[...].astype(F32)
    quarter = kept.shape[0]
    kept[...] = total[quarter:].astype(kept.dtype)
    step = pl.program_id(0)

    @pl.when(step < LEFT)
    def _():
        left[...] = total[:quarter].astype(BF16)

    @pl.when(step >= LEFT)
    def _():
        right[...] = total[:quarter].astype(BF16)


def call_pair_sum(own, got, tile=1024):
    half, width = own.shape
    steps = width // tile
    out = (half // 2, tile)
    *sent, kept = pl.pallas_call(
        pair_sum,
        grid=(steps,),
        in_specs=[pl.BlockSpec((half, tile), lambda j: (0, j))] * 2,
        out_specs=[
            pl.BlockSpec(out, lambda j: (0, jnp.minimum(j, LEFT - 1))),
            pl.BlockSpec(out, lambda j: (0, jnp.maximum(j - LEFT, 0))),
            pl.BlockSpec(out, lambda j: (0, j)),
        ],
        out_shape=[
            jax.ShapeDtypeStruct((half // 2, LEFT * tile), BF16),
            jax.ShapeDtypeStruct((half // 2, width - LEFT * tile), BF16),
            jax.ShapeDtypeStruct((half // 2, width), KEPT),
        ],
        compiler_params=params(12),
        name="pair_sum",
        cost_estimate=cost(half * width, half * width * 6),
    )(own, got)
    return sent, kept


def quad_sum(kept, left, right, one, two, three, own):
    share = own.shape[0]
    cut = left.shape[1]
    for k, out in enumerate((one, two, three, own)):
        rows = slice(k * share, (k + 1) * share)
        out[:, :cut] = (kept[rows, :cut].astype(F32) + left[rows, :].astype(F32)).astype(out.dtype)
        out[:, cut:] = (kept[rows, cut:].astype(F32) + right[rows, :].astype(F32)).astype(out.dtype)


def call_quad_sum(kept, got):
    quarter, width = kept.shape
    share = quarter // 4
    return pl.pallas_call(
        quad_sum,
        in_specs=[VMEM] * 3,
        out_specs=[VMEM] * 4,
        out_shape=[jax.ShapeDtypeStruct((share, width), BF16)] * 3
        + [jax.ShapeDtypeStruct((share, width), F32)],
        compiler_params=params(60),
        name="quad_sum",
        cost_estimate=cost(quarter * width, quarter * width * 8),
    )(kept, *got)


def reorder(order, inner, out, flat):
    count, share, channels = inner.shape
    block = order.shape[1]
    per = channels // block
    tiles = count * per
    for t in range(tiles):
        flat[t] = inner[t // per, :, (t % per) * block : (t % per + 1) * block].astype(F32)

    def one(j):
        wanted = jnp.broadcast_to(order[pl.ds(j, 1), :], (share, block))
        lane = wanted % block
        tile = wanted // block
        total = jnp.zeros((share, block), F32)
        for t in range(tiles):
            found = jnp.take_along_axis(flat[t], lane, axis=1, mode="promise_in_bounds")
            total = jnp.where(tile == t, found, total)
        return total.astype(BF16)

    def group(g, _):
        for i in range(per):
            out[g, :, i * block : (i + 1) * block] = one(g * per + i)
        return 0

    lax.fori_loop(0, count, group, 0)


def call_reorder(order, inner):
    count, share, channels = inner.shape
    tiles, block = order.shape
    return pl.pallas_call(
        reorder,
        in_specs=[VMEM] * 2,
        out_specs=VMEM,
        out_shape=jax.ShapeDtypeStruct(inner.shape, BF16),
        scratch_shapes=[pltpu.VMEM((tiles, share, block), F32)],
        compiler_params=params(6),
        name="reorder",
        cost_estimate=cost(tiles * tiles * share * block * 4, count * share * channels * 4),
    )(order, inner)


def sources():
    core, zh, y = place_of()
    found = []
    for c in range(2):
        for slot, (chunk, row, back) in enumerate(HELD):
            cc = core if c == 0 else 1 - core
            zz = zh if slot % 2 == 0 else 1 - zh
            place = zz * 8 + lax.rem(y + 4 - back, 4) * 2 + cc
            found.append((c * 5 + chunk, row, place))
    return found


def block_of(ref, z, i, share, block, base=0):
    each = block // share
    parts = [
        ref[z * share : (z + 1) * share, base + (i * each + q) * block : base + (i * each + q + 1) * block]
        for q in range(each)
    ]
    return jnp.concatenate(parts, axis=0)


def delta_rows(mixed, *refs):
    chunks, out = refs[:CHUNKS], refs[CHUNKS]
    share = out.shape[0]
    block = mixed.shape[2] // 2
    for chunk, z, g in sources():
        for i in range(2):
            cols = pl.ds(pl.multiple_of((g * 2 + i) * block, block), block)
            factor = block_of(chunks[chunk], z, i, share, block)
            out[:, cols] = dot(mixed[g, :, i * block : (i + 1) * block], factor)


def call_delta_rows(mixed, chunks):
    groups, share, channels = mixed.shape
    width = groups * channels
    per = chunks[0].shape[1] - width
    second = [pl.BlockSpec((v.shape[0], per), lambda j: (0, width // per)) for v in chunks]
    return pl.pallas_call(
        delta_rows,
        grid=(1,),
        in_specs=[pl.BlockSpec(mixed.shape, lambda j: (0, 0, 0))] + second,
        out_specs=pl.BlockSpec((share, width), lambda j: (0, 0)),
        out_shape=jax.ShapeDtypeStruct((share, width), F32),
        compiler_params=params(60),
        name="delta_rows",
        cost_estimate=cost(share * width * channels, share * width * 6),
    )(mixed, *chunks)


def factor_grads(order, mixed, tokens_t, *refs):
    chunks, refs = refs[:CHUNKS], refs[CHUNKS:]
    d_inner, sums, cot_out, cot, routed, second, sem, cot_sems, second_sems = refs
    core, zh, y = place_of()
    block = order.shape[1]
    rows, channels = d_inner.shape
    share = rows // 16
    width = cot.shape[1]
    hidden = tokens_t.shape[0]
    found = sources()
    place = zh * 8 + y * 2 + core
    second_copies, cot_copies = [], []
    for k, (chunk, z, g) in enumerate(found):
        held = chunks[chunk].at[z * share : (z + 1) * share, :]
        rows_of = pl.ds(pl.multiple_of(g * share, share), share)
        second_copies.append(
            pltpu.make_async_copy(held.at[:, width:], second.at[k], second_sems.at[k])
        )
        cot_copies.append(
            pltpu.make_async_copy(held.at[:, :width], cot.at[rows_of, :], cot_sems.at[k])
        )
    for copy in second_copies + cot_copies:
        copy.start()
    row = lax.broadcasted_iota(jnp.int32, (channels, block), 0) + place * channels
    each = block // share
    for k, (chunk, z, g) in enumerate(found):
        second_copies[k].wait()
        for i in range(2):
            n = g * 2 + i
            hits = jnp.where(row == order[pl.ds(n, 1), :], 1.0, 0.0).astype(BF16)
            factor = jnp.concatenate(
                [second[k, :, q * block : (q + 1) * block] for q in range(i * each, (i + 1) * each)],
                axis=0,
            )
            cols = pl.ds(pl.multiple_of(n * block, block), block)
            routed[:, cols] = dot(hits, factor).astype(BF16)
    for copy in cot_copies:
        copy.wait()
    copy = pltpu.make_async_copy(cot, cot_out, sem)
    copy.start()
    grad = dot_nt(cot[...], routed[...]).astype(BF16)
    d_inner[...] = grad
    whole = dot(tokens_t[...], grad)
    unit = lax.broadcasted_iota(jnp.int32, (hidden, block), 0)
    d_first = jnp.where(unit < hidden // 2, whole[:, :block], whole[:, block:]).astype(BF16)
    each = sums.shape[0] // 8
    few = channels // 8
    room = each - few
    for k in range(8):
        have = min(room, hidden - k * room)
        if have < room:
            sums[k * each : k * each + room, :] = jnp.zeros((room, block), BF16)
        sums[k * each : k * each + have, :] = d_first[k * room : k * room + have]
    mixed_t = mixed[...].reshape(rows, channels).T
    for i in range(channels // block):
        n = place * 2 + i
        cols = pl.ds(pl.multiple_of(n * block, block), block)
        d_second = dot(mixed_t[i * block : (i + 1) * block, :], cot[:, cols]).astype(BF16)
        for q in range(block // few):
            k = i * (block // few) + q
            sums[k * each + room : (k + 1) * each, :] = d_second[q * few : (q + 1) * few]
    copy.wait()


def call_factor_grads(order, mixed, tokens_t, chunks, room):
    groups, share, channels = mixed.shape
    rows = groups * share
    tiles, block = order.shape
    width = tiles * block
    each = room + channels // 8
    return pl.pallas_call(
        factor_grads,
        in_specs=[VMEM] * 3 + [ANY] * CHUNKS,
        out_specs=[VMEM, VMEM, ANY],
        out_shape=[
            jax.ShapeDtypeStruct((rows, channels), BF16),
            jax.ShapeDtypeStruct((8 * each, block), BF16),
            jax.ShapeDtypeStruct((rows, width), BF16),
        ],
        scratch_shapes=[
            pltpu.VMEM((rows, width), BF16),
            pltpu.VMEM((channels, width), BF16),
            pltpu.VMEM((16, share, 2 * block * block // share), BF16),
            pltpu.SemaphoreType.DMA,
            pltpu.SemaphoreType.DMA((16,)),
            pltpu.SemaphoreType.DMA((16,)),
        ],
        compiler_params=params(60),
        name="factor_grads",
        cost_estimate=cost(4 * rows * channels * width, rows * width * 2),
    )(order, mixed, tokens_t, *chunks)


def token_grads(weight, cot, factor, d_inner, out, weight_held, cot_held, weight_sems, cot_sems):
    steps = weight_sems.shape[0]
    tile = weight.shape[1] // steps
    cols = [slice(k * tile, (k + 1) * tile) for k in range(steps)]
    copies = []
    for k, c in enumerate(cols):
        copies.append(pltpu.make_async_copy(cot.at[:, c], cot_held.at[:, c], cot_sems.at[k]))
        copies.append(pltpu.make_async_copy(weight.at[:, c], weight_held.at[:, c], weight_sems.at[k]))
    for copy in copies:
        copy.start()
    hidden, block = factor.shape
    unit = lax.broadcasted_iota(jnp.int32, (hidden, block), 0)
    zero = jnp.zeros((hidden, block), BF16)
    first = jnp.where(unit < hidden // 2, factor[...], zero)
    second = jnp.where(unit < hidden // 2, zero, factor[...])
    out[...] = dot_nt(jnp.concatenate([first, second], axis=1), d_inner[...])
    for k, c in enumerate(cols):
        copies[2 * k].wait()
        copies[2 * k + 1].wait()
        out[...] += dot_nt(weight_held[:, c], cot_held[:, c])


def call_token_grads(weight, cot, factor, d_inner, tile=1024):
    hidden, width = weight.shape
    rows, channels = d_inner.shape
    return pl.pallas_call(
        token_grads,
        in_specs=[ANY, ANY, VMEM, VMEM],
        out_specs=VMEM,
        out_shape=jax.ShapeDtypeStruct((hidden, rows), F32),
        scratch_shapes=[
            pltpu.VMEM((hidden, width), BF16),
            pltpu.VMEM((rows, width), BF16),
            pltpu.SemaphoreType.DMA((width // tile,)),
            pltpu.SemaphoreType.DMA((width // tile,)),
        ],
        compiler_params=params(60),
        name="token_grads",
        cost_estimate=cost(2 * rows * hidden * width, hidden * width * 2),
    )(weight, cot, factor, d_inner)


def per_device(tokens, base_weight, first_factor, second_factor, channel_order, cotangent):
    rows, hidden = tokens.shape
    blocks, block_in, block_out = first_factor.shape
    width = base_weight.shape[1]
    channels = blocks * block_out
    share = rows // 16
    room = -(-hidden // 128) * 16
    hold = lax.optimization_barrier
    order = channel_order.reshape(-1, block_out)

    bundle = call_pack(cotangent, second_factor.reshape(channels, block_out))
    partner = lax.ppermute(bundle, "zh", SWAP)
    factor = first_factor.reshape(hidden, block_out)
    block = jnp.arange(hidden, dtype=jnp.int32)[:, None] // block_in
    wide = jnp.concatenate([jnp.where(block == n, factor, 0) for n in range(blocks)], axis=1)
    inner = dot(tokens, wide).astype(BF16).reshape(16, share, channels)
    inner = lax.all_to_all(inner, TENSOR, 0, 0)
    other, own = call_base_rows(tokens, base_weight)
    bundle, partner, factor, inner, other, own = hold((bundle, partner, factor, inner, other, own))

    pair = jnp.concatenate([bundle, partner], axis=0)
    next_y, last_y = turn(pair, 1), turn(pair, 3)
    mixed = call_reorder(order, inner)
    sent, kept = call_pair_sum(own, lax.ppermute(other, "c", SWAP))
    left = lax.ppermute(sent[0], "zh", SWAP)
    theirs = [lax.ppermute(pair, "c", SWAP)]
    pair, next_y, last_y, mixed, left, right, kept, theirs = hold(
        (pair, next_y, last_y, mixed, left, sent[1], kept, theirs)
    )

    far = [turn(next_y[:share], 1), turn(last_y[share:], 3)]
    mine = [pair, next_y, last_y]
    theirs = theirs + [lax.ppermute(v, "c", SWAP) for v in mine[1:]]
    mixed_mine = lax.all_to_all(mixed, TENSOR, 0, 0)
    far, theirs, left, right, mixed_mine = hold((far, theirs, left, right, mixed_mine))

    right = lax.ppermute(right, "zh", SWAP)
    chunks = mine + far + theirs + [lax.ppermute(v, "c", SWAP) for v in far]
    d_inner, sums, cot = call_factor_grads(order, mixed_mine, tokens.T, chunks, room)
    sums = lax.all_to_all(sums.reshape(8, -1, block_out), DP, 0, 0)
    terms = call_quad_sum(kept, [left, right])
    delta = call_delta_rows(mixed, chunks)
    terms, sums, cot, delta = hold((terms, sums, cot, delta))

    parts = [turn(terms[d - 1], d) for d in (1, 2, 3)]
    sums = jnp.sum(sums.astype(F32), axis=0).astype(BF16)
    final = spread(sums, DP, 8)
    d_tokens = call_token_grads(base_weight, cot, factor, d_inner).T
    parts, d_tokens = hold((parts, d_tokens))

    output = terms[3] + delta
    for part in parts:
        output = output + part.astype(F32)
    d_first = final[:, :room].reshape(-1, block_out)[:hidden].astype(F32)
    d_second = final[:, room:].astype(F32)
    return (
        output,
        d_tokens,
        d_first.reshape(blocks, block_in, block_out),
        d_second.reshape(blocks, block_out, block_out),
    )


def solution(mesh):
    fine = Mesh(mesh.devices.reshape(2, 4, 2, 4, 2), ("zl", "x", "zh", "y", "c"))
    return jax.shard_map(
        per_device,
        mesh=fine,
        in_specs=(
            P(DP, TENSOR),
            P(TENSOR, None),
            P(TENSOR, None, None),
            P(TENSOR, None, None),
            P(),
            P(DP + TENSOR, None),
        ),
        out_specs=(
            P(DP + TENSOR, None),
            P(DP, TENSOR),
            P(TENSOR, None, None),
            P(TENSOR, None, None),
        ),
        check_vma=False,
    )
```

```python
import jax
import jax.numpy as jnp
from jax import lax
from jax.experimental import pallas as pl
from jax.experimental.pallas import tpu as pltpu
from jax.sharding import Mesh, PartitionSpec as P

F32 = jnp.float32
BF16 = jnp.bfloat16
DP = ("zl", "x")
TENSOR = ("zh", "y", "c")
SWAP = [(0, 1), (1, 0)]
TURNS = (1, 3, 2)
VMEM = pl.BlockSpec(memory_space=pltpu.VMEM)
ANY = pl.BlockSpec(memory_space=pl.ANY)
MIB = 1 << 20
CHUNKS = 10
HELD = ((0, 0, 0), (0, 1, 0), (1, 0, 1), (1, 1, 1), (2, 0, 3), (2, 1, 3), (3, 0, 2), (4, 0, 2))
SCALE = 100
KEPT = BF16
LEFT = 2
TILE = 2048


def params(mib):
    return pltpu.CompilerParams(vmem_limit_bytes=mib * MIB)


def cost(flops, moved):
    return pl.CostEstimate(flops=flops // SCALE, bytes_accessed=moved // SCALE, transcendentals=0)


def turn(value, by):
    return lax.ppermute(value, "y", [(i, (i + by) % 4) for i in range(4)])


def spread(value, axes, count):
    whole = jnp.broadcast_to(value[None], (count,) + value.shape)
    return lax.all_to_all(whole, axes, 0, 0)


def place_of():
    return lax.axis_index("c"), lax.axis_index("zh"), lax.axis_index("y")


def dot(a, b):
    return jnp.dot(a, b, preferred_element_type=F32)


def dot_nt(a, b):
    return lax.dot_general(a, b, (((1,), (1,)), ((), ())), preferred_element_type=F32)


def pack(cotangent, second, out):
    share, width = cotangent.shape
    block = second.shape[1]
    out[:, :width] = cotangent[...]
    for q in range(second.shape[0] // share):
        out[:, width + q * block : width + (q + 1) * block] = second[q * share : (q + 1) * share, :]


def call_pack(cotangent, second):
    share, width = cotangent.shape
    return pl.pallas_call(
        pack,
        in_specs=[VMEM] * 2,
        out_specs=VMEM,
        out_shape=jax.ShapeDtypeStruct((share, width + second.size // share), BF16),
        compiler_params=params(60),
        name="pack",
        cost_estimate=cost(share, share * width * 4),
    )(cotangent, second)


def base_rows(tokens, weight, other, own, held):
    step = pl.program_id(0)
    share = tokens.shape[0] // 16
    half = tokens.shape[0] // 2

    @pl.when(step == 0)
    def _():
        core, zh, y = place_of()
        for p in range(2):
            for z in range(2):
                for k in range(4):
                    c = 1 - core if p == 0 else core
                    zz = 1 - zh if z == 0 else zh
                    g = zz * 8 + lax.rem(y + (k + 1) % 4, 4) * 2 + c
                    at = p * half + (z * 4 + k) * share
                    held[at : at + share, :] = tokens[pl.ds(pl.multiple_of(g * share, share), share), :]

    total = dot(held[...], weight[...])
    other[...] = total[:half].astype(BF16)
    own[...] = total[half:].astype(own.dtype)


def call_base_rows(tokens, weight, tile=1024):
    rows, hidden = tokens.shape
    width = weight.shape[1]
    half = rows // 2
    return pl.pallas_call(
        base_rows,
        grid=(width // tile,),
        in_specs=[
            pl.BlockSpec((rows, hidden), lambda j: (0, 0)),
            pl.BlockSpec((hidden, tile), lambda j: (0, j)),
        ],
        out_specs=[pl.BlockSpec((half, tile), lambda j: (0, j))] * 2,
        out_shape=[
            jax.ShapeDtypeStruct((half, width), BF16),
            jax.ShapeDtypeStruct((half, width), KEPT),
        ],
        scratch_shapes=[pltpu.VMEM((rows, hidden), BF16)],
        compiler_params=params(60),
        name="base_rows",
        cost_estimate=cost(2 * rows * hidden * width, hidden * width * 2),
    )(tokens, weight)


def pair_sum(own, got, left, right, kept):
    total = own[...].astype(F32) + got[...].astype(F32)
    quarter = kept.shape[0]
    kept[...] = total[quarter:].astype(kept.dtype)
    step = pl.program_id(0)

    @pl.when(step < LEFT)
    def _():
        left[...] = total[:quarter].astype(BF16)

    @pl.when(step >= LEFT)
    def _():
        right[...] = total[:quarter].astype(BF16)


def call_pair_sum(own, got, tile=1024):
    half, width = own.shape
    steps = width // tile
    out = (half // 2, tile)
    *sent, kept = pl.pallas_call(
        pair_sum,
        grid=(steps,),
        in_specs=[pl.BlockSpec((half, tile), lambda j: (0, j))] * 2,
        out_specs=[
            pl.BlockSpec(out, lambda j: (0, jnp.minimum(j, LEFT - 1))),
            pl.BlockSpec(out, lambda j: (0, jnp.maximum(j - LEFT, 0))),
            pl.BlockSpec(out, lambda j: (0, j)),
        ],
        out_shape=[
            jax.ShapeDtypeStruct((half // 2, LEFT * tile), BF16),
            jax.ShapeDtypeStruct((half // 2, width - LEFT * tile), BF16),
            jax.ShapeDtypeStruct((half // 2, width), KEPT),
        ],
        compiler_params=params(12),
        name="pair_sum",
        cost_estimate=cost(half * width, half * width * 6),
    )(own, got)
    return sent, kept


def quad_sum(kept, left, right, one, two, three, own):
    share = own.shape[0]
    cut = left.shape[1]
    for k, out in enumerate((one, two, three, own)):
        rows = slice(k * share, (k + 1) * share)
        out[:, :cut] = (kept[rows, :cut].astype(F32) + left[rows, :].astype(F32)).astype(out.dtype)
        out[:, cut:] = (kept[rows, cut:].astype(F32) + right[rows, :].astype(F32)).astype(out.dtype)


def call_quad_sum(kept, got):
    quarter, width = kept.shape
    share = quarter // 4
    return pl.pallas_call(
        quad_sum,
        in_specs=[VMEM] * 3,
        out_specs=[VMEM] * 4,
        out_shape=[jax.ShapeDtypeStruct((share, width), BF16)] * 3
        + [jax.ShapeDtypeStruct((share, width), F32)],
        compiler_params=params(60),
        name="quad_sum",
        cost_estimate=cost(quarter * width, quarter * width * 8),
    )(kept, *got)


def reorder(order, inner, out, flat):
    count, share, channels = inner.shape
    block = order.shape[1]
    per = channels // block
    tiles = count * per
    for t in range(tiles):
        flat[t] = inner[t // per, :, (t % per) * block : (t % per + 1) * block].astype(F32)

    def one(j):
        wanted = jnp.broadcast_to(order[pl.ds(j, 1), :], (share, block))
        lane = wanted % block
        tile = wanted // block
        total = jnp.zeros((share, block), F32)
        for t in range(tiles):
            found = jnp.take_along_axis(flat[t], lane, axis=1, mode="promise_in_bounds")
            total = jnp.where(tile == t, found, total)
        return total.astype(BF16)

    def group(g, _):
        for i in range(per):
            out[g, :, i * block : (i + 1) * block] = one(g * per + i)
        return 0

    lax.fori_loop(0, count, group, 0)


def call_reorder(order, inner):
    count, share, channels = inner.shape
    tiles, block = order.shape
    return pl.pallas_call(
        reorder,
        in_specs=[VMEM] * 2,
        out_specs=VMEM,
        out_shape=jax.ShapeDtypeStruct(inner.shape, BF16),
        scratch_shapes=[pltpu.VMEM((tiles, share, block), F32)],
        compiler_params=params(6),
        name="reorder",
        cost_estimate=cost(tiles * tiles * share * block * 4, count * share * channels * 4),
    )(order, inner)


def sources():
    core, zh, y = place_of()
    found = []
    for c in range(2):
        for slot, (chunk, row, back) in enumerate(HELD):
            cc = core if c == 0 else 1 - core
            zz = zh if slot % 2 == 0 else 1 - zh
            place = zz * 8 + lax.rem(y + 4 - back, 4) * 2 + cc
            found.append((c * 5 + chunk, row, place))
    return found


def block_of(ref, z, i, share, block, base=0):
    each = block // share
    parts = [
        ref[z * share : (z + 1) * share, base + (i * each + q) * block : base + (i * each + q + 1) * block]
        for q in range(each)
    ]
    return jnp.concatenate(parts, axis=0)


def delta_rows(mixed, *refs):
    chunks, out = refs[:CHUNKS], refs[CHUNKS]
    share = out.shape[0]
    block = mixed.shape[2] // 2
    for chunk, z, g in sources():
        for i in range(2):
            cols = pl.ds(pl.multiple_of((g * 2 + i) * block, block), block)
            factor = block_of(chunks[chunk], z, i, share, block)
            out[:, cols] = dot(mixed[g, :, i * block : (i + 1) * block], factor)


def call_delta_rows(mixed, chunks):
    groups, share, channels = mixed.shape
    width = groups * channels
    per = chunks[0].shape[1] - width
    second = [pl.BlockSpec((v.shape[0], per), lambda j: (0, width // per)) for v in chunks]
    return pl.pallas_call(
        delta_rows,
        grid=(1,),
        in_specs=[pl.BlockSpec(mixed.shape, lambda j: (0, 0, 0))] + second,
        out_specs=pl.BlockSpec((share, width), lambda j: (0, 0)),
        out_shape=jax.ShapeDtypeStruct((share, width), F32),
        compiler_params=params(60),
        name="delta_rows",
        cost_estimate=cost(share * width * channels, share * width * 6),
    )(mixed, *chunks)


def factor_grads(order, mixed, tokens_t, *refs):
    chunks, (d_inner, sums, cot_out, cot, routed, sem) = refs[:CHUNKS], refs[CHUNKS:]
    core, zh, y = place_of()
    block = order.shape[1]
    rows, channels = d_inner.shape
    share = rows // 16
    width = cot.shape[1]
    hidden = tokens_t.shape[0]
    found = sources()
    place = zh * 8 + y * 2 + core
    row = lax.broadcasted_iota(jnp.int32, (channels, block), 0) + place * channels
    for chunk, z, g in found:
        cot[pl.ds(pl.multiple_of(g * share, share), share), :] = chunks[chunk][
            z * share : (z + 1) * share, :width
        ]
        for i in range(2):
            n = g * 2 + i
            hits = jnp.where(row == order[pl.ds(n, 1), :], 1.0, 0.0).astype(BF16)
            factor = block_of(chunks[chunk], z, i, share, block, width)
            cols = pl.ds(pl.multiple_of(n * block, block), block)
            routed[:, cols] = dot(hits, factor).astype(BF16)
    copy = pltpu.make_async_copy(cot, cot_out, sem)
    copy.start()
    grad = dot_nt(cot[...], routed[...]).astype(BF16)
    d_inner[...] = grad
    whole = dot(tokens_t[...], grad)
    unit = lax.broadcasted_iota(jnp.int32, (hidden, block), 0)
    d_first = jnp.where(unit < hidden // 2, whole[:, :block], whole[:, block:]).astype(BF16)
    each = sums.shape[0] // 8
    few = channels // 8
    room = each - few
    for k in range(8):
        have = min(room, hidden - k * room)
        if have < room:
            sums[k * each : k * each + room, :] = jnp.zeros((room, block), BF16)
        sums[k * each : k * each + have, :] = d_first[k * room : k * room + have]
    mixed_t = mixed[...].reshape(rows, channels).T
    for i in range(channels // block):
        n = place * 2 + i
        cols = pl.ds(pl.multiple_of(n * block, block), block)
        d_second = dot(mixed_t[i * block : (i + 1) * block, :], cot[:, cols]).astype(BF16)
        for q in range(block // few):
            k = i * (block // few) + q
            sums[k * each + room : (k + 1) * each, :] = d_second[q * few : (q + 1) * few]
    copy.wait()


def call_factor_grads(order, mixed, tokens_t, chunks, room):
    groups, share, channels = mixed.shape
    rows = groups * share
    tiles, block = order.shape
    width = tiles * block
    each = room + channels // 8
    return pl.pallas_call(
        factor_grads,
        in_specs=[VMEM] * (3 + CHUNKS),
        out_specs=[VMEM, VMEM, ANY],
        out_shape=[
            jax.ShapeDtypeStruct((rows, channels), BF16),
            jax.ShapeDtypeStruct((8 * each, block), BF16),
            jax.ShapeDtypeStruct((rows, width), BF16),
        ],
        scratch_shapes=[
            pltpu.VMEM((rows, width), BF16),
            pltpu.VMEM((channels, width), BF16),
            pltpu.SemaphoreType.DMA,
        ],
        compiler_params=params(26),
        name="factor_grads",
        cost_estimate=cost(4 * rows * channels * width, rows * width * 2),
    )(order, mixed, tokens_t, *chunks)


def token_grads(weight, cot, factor, d_inner, out):
    term = dot_nt(weight[...], cot[...])

    @pl.when(pl.program_id(0) == 0)
    def _():
        hidden, block = factor.shape
        unit = lax.broadcasted_iota(jnp.int32, (hidden, block), 0)
        zero = jnp.zeros((hidden, block), BF16)
        first = jnp.where(unit < hidden // 2, factor[...], zero)
        second = jnp.where(unit < hidden // 2, zero, factor[...])
        wide = jnp.concatenate([first, second], axis=1)
        out[...] = term + dot_nt(wide, d_inner[...])

    @pl.when(pl.program_id(0) > 0)
    def _():
        out[...] += term


def call_token_grads(weight, cot, factor, d_inner, tile=TILE):
    hidden, width = weight.shape
    rows, channels = d_inner.shape
    return pl.pallas_call(
        token_grads,
        grid=(width // tile,),
        in_specs=[
            pl.BlockSpec((hidden, tile), lambda k: (0, k)),
            pl.BlockSpec((rows, tile), lambda k: (0, k)),
            pl.BlockSpec(factor.shape, lambda k: (0, 0)),
            pl.BlockSpec((rows, channels), lambda k: (0, 0)),
        ],
        out_specs=pl.BlockSpec((hidden, rows), lambda k: (0, 0)),
        out_shape=jax.ShapeDtypeStruct((hidden, rows), F32),
        compiler_params=params(60),
        name="token_grads",
        cost_estimate=cost(2 * rows * hidden * width, hidden * width * 2),
    )(weight, cot, factor, d_inner)


def per_device(tokens, base_weight, first_factor, second_factor, channel_order, cotangent):
    rows, hidden = tokens.shape
    blocks, block_in, block_out = first_factor.shape
    width = base_weight.shape[1]
    channels = blocks * block_out
    share = rows // 16
    room = -(-hidden // 128) * 16
    hold = lax.optimization_barrier
    order = channel_order.reshape(-1, block_out)

    bundle = call_pack(cotangent, second_factor.reshape(channels, block_out))
    partner = lax.ppermute(bundle, "zh", SWAP)
    factor = first_factor.reshape(hidden, block_out)
    block = jnp.arange(hidden, dtype=jnp.int32)[:, None] // block_in
    wide = jnp.concatenate([jnp.where(block == n, factor, 0) for n in range(blocks)], axis=1)
    inner = dot(tokens, wide).astype(BF16).reshape(16, share, channels)
    inner = lax.all_to_all(inner, TENSOR, 0, 0)
    other, own = call_base_rows(tokens, base_weight)
    bundle, partner, factor, inner, other, own = hold((bundle, partner, factor, inner, other, own))

    pair = jnp.concatenate([bundle, partner], axis=0)
    next_y, last_y = turn(pair, 1), turn(pair, 3)
    mixed = call_reorder(order, inner)
    sent, kept = call_pair_sum(own, lax.ppermute(other, "c", SWAP))
    theirs = [lax.ppermute(pair, "c", SWAP)]
    pair, next_y, last_y, mixed, sent, kept, theirs = hold(
        (pair, next_y, last_y, mixed, sent, kept, theirs)
    )

    far = [turn(next_y[:share], 1), turn(last_y[share:], 3)]
    mine = [pair, next_y, last_y]
    theirs = theirs + [lax.ppermute(v, "c", SWAP) for v in mine[1:]]
    mixed_mine = lax.all_to_all(mixed, TENSOR, 0, 0)
    left = lax.ppermute(sent[0], "zh", SWAP)
    far, theirs, left, right, mixed_mine = hold((far, theirs, left, sent[1], mixed_mine))

    right = lax.ppermute(right, "zh", SWAP)
    chunks = mine + far + theirs + [lax.ppermute(v, "c", SWAP) for v in far]
    d_inner, sums, cot = call_factor_grads(order, mixed_mine, tokens.T, chunks, room)
    sums = lax.all_to_all(sums.reshape(8, -1, block_out), DP, 0, 0)
    terms = call_quad_sum(kept, [left, right])
    delta = call_delta_rows(mixed, chunks)
    terms, sums, cot, delta = hold((terms, sums, cot, delta))

    parts = [turn(terms[d - 1], d) for d in (1, 2, 3)]
    sums = jnp.sum(sums.astype(F32), axis=0).astype(BF16)
    final = spread(sums, DP, 8)
    d_tokens = call_token_grads(base_weight, cot, factor, d_inner).T
    parts, d_tokens = hold((parts, d_tokens))

    output = terms[3] + delta
    for part in parts:
        output = output + part.astype(F32)
    d_first = final[:, :room].reshape(-1, block_out)[:hidden].astype(F32)
    d_second = final[:, room:].astype(F32)
    return (
        output,
        d_tokens,
        d_first.reshape(blocks, block_in, block_out),
        d_second.reshape(blocks, block_out, block_out),
    )


def solution(mesh):
    fine = Mesh(mesh.devices.reshape(2, 4, 2, 4, 2), ("zl", "x", "zh", "y", "c"))
    return jax.shard_map(
        per_device,
        mesh=fine,
        in_specs=(
            P(DP, TENSOR),
            P(TENSOR, None),
            P(TENSOR, None, None),
            P(TENSOR, None, None),
            P(),
            P(DP + TENSOR, None),
        ),
        out_specs=(
            P(DP + TENSOR, None),
            P(DP, TENSOR),
            P(TENSOR, None, None),
            P(TENSOR, None, None),
        ),
        check_vma=False,
    )
```

```python
import jax
import jax.numpy as jnp
from jax import lax
from jax.experimental import pallas as pl
from jax.experimental.pallas import tpu as pltpu
from jax.sharding import Mesh, PartitionSpec as P

F32 = jnp.float32
BF16 = jnp.bfloat16
DP = ("zl", "x")
TENSOR = ("zh", "y", "c")
SWAP = [(0, 1), (1, 0)]
TURNS = (1, 3, 2)
VMEM = pl.BlockSpec(memory_space=pltpu.VMEM)
ANY = pl.BlockSpec(memory_space=pl.ANY)
MIB = 1 << 20
CHUNKS = 10
HELD = ((0, 0, 0), (0, 1, 0), (1, 0, 1), (1, 1, 1), (2, 0, 3), (2, 1, 3), (3, 0, 2), (4, 0, 2))
SCALE = 100
KEPT = BF16
LEFT = 3
TILE = 2048


def params(mib):
    return pltpu.CompilerParams(vmem_limit_bytes=mib * MIB)


def cost(flops, moved):
    return pl.CostEstimate(flops=flops // SCALE, bytes_accessed=moved // SCALE, transcendentals=0)


def turn(value, by):
    return lax.ppermute(value, "y", [(i, (i + by) % 4) for i in range(4)])


def spread(value, axes, count):
    whole = jnp.broadcast_to(value[None], (count,) + value.shape)
    return lax.all_to_all(whole, axes, 0, 0)


def place_of():
    return lax.axis_index("c"), lax.axis_index("zh"), lax.axis_index("y")


def dot(a, b):
    return jnp.dot(a, b, preferred_element_type=F32)


def dot_nt(a, b):
    return lax.dot_general(a, b, (((1,), (1,)), ((), ())), preferred_element_type=F32)


def pack(cotangent, second, out):
    share, width = cotangent.shape
    block = second.shape[1]
    out[:, :width] = cotangent[...]
    for q in range(second.shape[0] // share):
        out[:, width + q * block : width + (q + 1) * block] = second[q * share : (q + 1) * share, :]


def call_pack(cotangent, second):
    share, width = cotangent.shape
    return pl.pallas_call(
        pack,
        in_specs=[VMEM] * 2,
        out_specs=VMEM,
        out_shape=jax.ShapeDtypeStruct((share, width + second.size // share), BF16),
        compiler_params=params(60),
        name="pack",
        cost_estimate=cost(share, share * width * 4),
    )(cotangent, second)


def base_rows(tokens, weight, other, own, held):
    step = pl.program_id(0)
    share = tokens.shape[0] // 16
    half = tokens.shape[0] // 2

    @pl.when(step == 0)
    def _():
        core, zh, y = place_of()
        for p in range(2):
            for z in range(2):
                for k in range(4):
                    c = 1 - core if p == 0 else core
                    zz = 1 - zh if z == 0 else zh
                    g = zz * 8 + lax.rem(y + (k + 1) % 4, 4) * 2 + c
                    at = p * half + (z * 4 + k) * share
                    held[at : at + share, :] = tokens[pl.ds(pl.multiple_of(g * share, share), share), :]

    total = dot(held[...], weight[...])
    other[...] = total[:half].astype(BF16)
    own[...] = total[half:].astype(own.dtype)


def call_base_rows(tokens, weight, tile=1024):
    rows, hidden = tokens.shape
    width = weight.shape[1]
    half = rows // 2
    return pl.pallas_call(
        base_rows,
        grid=(width // tile,),
        in_specs=[
            pl.BlockSpec((rows, hidden), lambda j: (0, 0)),
            pl.BlockSpec((hidden, tile), lambda j: (0, j)),
        ],
        out_specs=[pl.BlockSpec((half, tile), lambda j: (0, j))] * 2,
        out_shape=[
            jax.ShapeDtypeStruct((half, width), BF16),
            jax.ShapeDtypeStruct((half, width), KEPT),
        ],
        scratch_shapes=[pltpu.VMEM((rows, hidden), BF16)],
        compiler_params=params(60),
        name="base_rows",
        cost_estimate=cost(2 * rows * hidden * width, hidden * width * 2),
    )(tokens, weight)


def pair_sum(own, got, left, right, kept):
    total = own[...].astype(F32) + got[...].astype(F32)
    quarter = kept.shape[0]
    kept[...] = total[quarter:].astype(kept.dtype)
    step = pl.program_id(0)

    @pl.when(step < LEFT)
    def _():
        left[...] = total[:quarter].astype(BF16)

    @pl.when(step >= LEFT)
    def _():
        right[...] = total[:quarter].astype(BF16)


def call_pair_sum(own, got, tile=512):
    half, width = own.shape
    steps = width // tile
    out = (half // 2, tile)
    *sent, kept = pl.pallas_call(
        pair_sum,
        grid=(steps,),
        in_specs=[pl.BlockSpec((half, tile), lambda j: (0, j))] * 2,
        out_specs=[
            pl.BlockSpec(out, lambda j: (0, jnp.minimum(j, LEFT - 1))),
            pl.BlockSpec(out, lambda j: (0, jnp.maximum(j - LEFT, 0))),
            pl.BlockSpec(out, lambda j: (0, j)),
        ],
        out_shape=[
            jax.ShapeDtypeStruct((half // 2, LEFT * tile), BF16),
            jax.ShapeDtypeStruct((half // 2, width - LEFT * tile), BF16),
            jax.ShapeDtypeStruct((half // 2, width), KEPT),
        ],
        compiler_params=params(12),
        name="pair_sum",
        cost_estimate=cost(half * width, half * width * 6),
    )(own, got)
    return sent, kept


def quad_sum(kept, left, right, one, two, three, own):
    share = own.shape[0]
    cut = left.shape[1]
    for k, out in enumerate((one, two, three, own)):
        rows = slice(k * share, (k + 1) * share)
        out[:, :cut] = (kept[rows, :cut].astype(F32) + left[rows, :].astype(F32)).astype(out.dtype)
        out[:, cut:] = (kept[rows, cut:].astype(F32) + right[rows, :].astype(F32)).astype(out.dtype)


def call_quad_sum(kept, got):
    quarter, width = kept.shape
    share = quarter // 4
    return pl.pallas_call(
        quad_sum,
        in_specs=[VMEM] * 3,
        out_specs=[VMEM] * 4,
        out_shape=[jax.ShapeDtypeStruct((share, width), BF16)] * 3
        + [jax.ShapeDtypeStruct((share, width), F32)],
        compiler_params=params(60),
        name="quad_sum",
        cost_estimate=cost(quarter * width, quarter * width * 8),
    )(kept, *got)


def reorder(order, inner, out, flat):
    count, share, channels = inner.shape
    block = order.shape[1]
    per = channels // block
    tiles = count * per
    for t in range(tiles):
        flat[t] = inner[t // per, :, (t % per) * block : (t % per + 1) * block].astype(F32)

    def one(j):
        wanted = jnp.broadcast_to(order[pl.ds(j, 1), :], (share, block))
        lane = wanted % block
        tile = wanted // block
        total = jnp.zeros((share, block), F32)
        for t in range(tiles):
            found = jnp.take_along_axis(flat[t], lane, axis=1, mode="promise_in_bounds")
            total = jnp.where(tile == t, found, total)
        return total.astype(BF16)

    def group(g, _):
        for i in range(per):
            out[g, :, i * block : (i + 1) * block] = one(g * per + i)
        return 0

    lax.fori_loop(0, count, group, 0)


def call_reorder(order, inner):
    count, share, channels = inner.shape
    tiles, block = order.shape
    return pl.pallas_call(
        reorder,
        in_specs=[VMEM] * 2,
        out_specs=VMEM,
        out_shape=jax.ShapeDtypeStruct(inner.shape, BF16),
        scratch_shapes=[pltpu.VMEM((tiles, share, block), F32)],
        compiler_params=params(6),
        name="reorder",
        cost_estimate=cost(tiles * tiles * share * block * 4, count * share * channels * 4),
    )(order, inner)


def sources():
    core, zh, y = place_of()
    found = []
    for c in range(2):
        for slot, (chunk, row, back) in enumerate(HELD):
            cc = core if c == 0 else 1 - core
            zz = zh if slot % 2 == 0 else 1 - zh
            place = zz * 8 + lax.rem(y + 4 - back, 4) * 2 + cc
            found.append((c * 5 + chunk, row, place))
    return found


def block_of(ref, z, i, share, block, base=0):
    each = block // share
    parts = [
        ref[z * share : (z + 1) * share, base + (i * each + q) * block : base + (i * each + q + 1) * block]
        for q in range(each)
    ]
    return jnp.concatenate(parts, axis=0)


def delta_rows(mixed, *refs):
    chunks, out = refs[:CHUNKS], refs[CHUNKS]
    share = out.shape[0]
    block = mixed.shape[2] // 2
    for chunk, z, g in sources():
        for i in range(2):
            cols = pl.ds(pl.multiple_of((g * 2 + i) * block, block), block)
            factor = block_of(chunks[chunk], z, i, share, block)
            out[:, cols] = dot(mixed[g, :, i * block : (i + 1) * block], factor)


def call_delta_rows(mixed, chunks):
    groups, share, channels = mixed.shape
    width = groups * channels
    per = chunks[0].shape[1] - width
    second = [pl.BlockSpec((v.shape[0], per), lambda j: (0, width // per)) for v in chunks]
    return pl.pallas_call(
        delta_rows,
        grid=(1,),
        in_specs=[pl.BlockSpec(mixed.shape, lambda j: (0, 0, 0))] + second,
        out_specs=pl.BlockSpec((share, width), lambda j: (0, 0)),
        out_shape=jax.ShapeDtypeStruct((share, width), F32),
        compiler_params=params(60),
        name="delta_rows",
        cost_estimate=cost(share * width * channels, share * width * 6),
    )(mixed, *chunks)


def factor_grads(order, mixed, tokens_t, *refs):
    chunks, (d_inner, sums, cot_out, cot, routed, sem) = refs[:CHUNKS], refs[CHUNKS:]
    core, zh, y = place_of()
    block = order.shape[1]
    rows, channels = d_inner.shape
    share = rows // 16
    width = cot.shape[1]
    hidden = tokens_t.shape[0]
    found = sources()
    place = zh * 8 + y * 2 + core
    row = lax.broadcasted_iota(jnp.int32, (channels, block), 0) + place * channels
    for chunk, z, g in found:
        cot[pl.ds(pl.multiple_of(g * share, share), share), :] = chunks[chunk][
            z * share : (z + 1) * share, :width
        ]
        for i in range(2):
            n = g * 2 + i
            hits = jnp.where(row == order[pl.ds(n, 1), :], 1.0, 0.0).astype(BF16)
            factor = block_of(chunks[chunk], z, i, share, block, width)
            cols = pl.ds(pl.multiple_of(n * block, block), block)
            routed[:, cols] = dot(hits, factor).astype(BF16)
    copy = pltpu.make_async_copy(cot, cot_out, sem)
    copy.start()
    grad = dot_nt(cot[...], routed[...]).astype(BF16)
    d_inner[...] = grad
    whole = dot(tokens_t[...], grad)
    unit = lax.broadcasted_iota(jnp.int32, (hidden, block), 0)
    d_first = jnp.where(unit < hidden // 2, whole[:, :block], whole[:, block:]).astype(BF16)
    each = sums.shape[0] // 8
    few = channels // 8
    room = each - few
    for k in range(8):
        have = min(room, hidden - k * room)
        if have < room:
            sums[k * each : k * each + room, :] = jnp.zeros((room, block), BF16)
        sums[k * each : k * each + have, :] = d_first[k * room : k * room + have]
    mixed_t = mixed[...].reshape(rows, channels).T
    for i in range(channels // block):
        n = place * 2 + i
        cols = pl.ds(pl.multiple_of(n * block, block), block)
        d_second = dot(mixed_t[i * block : (i + 1) * block, :], cot[:, cols]).astype(BF16)
        for q in range(block // few):
            k = i * (block // few) + q
            sums[k * each + room : (k + 1) * each, :] = d_second[q * few : (q + 1) * few]
    copy.wait()


def call_factor_grads(order, mixed, tokens_t, chunks, room):
    groups, share, channels = mixed.shape
    rows = groups * share
    tiles, block = order.shape
    width = tiles * block
    each = room + channels // 8
    return pl.pallas_call(
        factor_grads,
        in_specs=[VMEM] * (3 + CHUNKS),
        out_specs=[VMEM, VMEM, ANY],
        out_shape=[
            jax.ShapeDtypeStruct((rows, channels), BF16),
            jax.ShapeDtypeStruct((8 * each, block), BF16),
            jax.ShapeDtypeStruct((rows, width), BF16),
        ],
        scratch_shapes=[
            pltpu.VMEM((rows, width), BF16),
            pltpu.VMEM((channels, width), BF16),
            pltpu.SemaphoreType.DMA,
        ],
        compiler_params=params(26),
        name="factor_grads",
        cost_estimate=cost(4 * rows * channels * width, rows * width * 2),
    )(order, mixed, tokens_t, *chunks)


def token_grads(weight, cot, factor, d_inner, out):
    term = dot_nt(weight[...], cot[...])

    @pl.when(pl.program_id(0) == 0)
    def _():
        hidden, block = factor.shape
        unit = lax.broadcasted_iota(jnp.int32, (hidden, block), 0)
        zero = jnp.zeros((hidden, block), BF16)
        first = jnp.where(unit < hidden // 2, factor[...], zero)
        second = jnp.where(unit < hidden // 2, zero, factor[...])
        wide = jnp.concatenate([first, second], axis=1)
        out[...] = term + dot_nt(wide, d_inner[...])

    @pl.when(pl.program_id(0) > 0)
    def _():
        out[...] += term


def call_token_grads(weight, cot, factor, d_inner, tile=TILE):
    hidden, width = weight.shape
    rows, channels = d_inner.shape
    return pl.pallas_call(
        token_grads,
        grid=(width // tile,),
        in_specs=[
            pl.BlockSpec((hidden, tile), lambda k: (0, k)),
            pl.BlockSpec((rows, tile), lambda k: (0, k)),
            pl.BlockSpec(factor.shape, lambda k: (0, 0)),
            pl.BlockSpec((rows, channels), lambda k: (0, 0)),
        ],
        out_specs=pl.BlockSpec((hidden, rows), lambda k: (0, 0)),
        out_shape=jax.ShapeDtypeStruct((hidden, rows), F32),
        compiler_params=params(60),
        name="token_grads",
        cost_estimate=cost(2 * rows * hidden * width, hidden * width * 2),
    )(weight, cot, factor, d_inner)


def per_device(tokens, base_weight, first_factor, second_factor, channel_order, cotangent):
    rows, hidden = tokens.shape
    blocks, block_in, block_out = first_factor.shape
    width = base_weight.shape[1]
    channels = blocks * block_out
    share = rows // 16
    room = -(-hidden // 128) * 16
    hold = lax.optimization_barrier
    order = channel_order.reshape(-1, block_out)

    bundle = call_pack(cotangent, second_factor.reshape(channels, block_out))
    partner = lax.ppermute(bundle, "zh", SWAP)
    factor = first_factor.reshape(hidden, block_out)
    block = jnp.arange(hidden, dtype=jnp.int32)[:, None] // block_in
    wide = jnp.concatenate([jnp.where(block == n, factor, 0) for n in range(blocks)], axis=1)
    inner = dot(tokens, wide).astype(BF16).reshape(16, share, channels)
    inner = lax.all_to_all(inner, TENSOR, 0, 0)
    other, own = call_base_rows(tokens, base_weight)
    bundle, partner, factor, inner, other, own = hold((bundle, partner, factor, inner, other, own))

    pair = jnp.concatenate([bundle, partner], axis=0)
    next_y, last_y = turn(pair, 1), turn(pair, 3)
    mixed = call_reorder(order, inner)
    sent, kept = call_pair_sum(own, lax.ppermute(other, "c", SWAP))
    theirs = [lax.ppermute(pair, "c", SWAP)]
    pair, next_y, last_y, mixed, sent, kept, theirs = hold(
        (pair, next_y, last_y, mixed, sent, kept, theirs)
    )

    far = [turn(next_y[:share], 1), turn(last_y[share:], 3)]
    mine = [pair, next_y, last_y]
    theirs = theirs + [lax.ppermute(v, "c", SWAP) for v in mine[1:]]
    mixed_mine = lax.all_to_all(mixed, TENSOR, 0, 0)
    left = lax.ppermute(sent[0], "zh", SWAP)
    far, theirs, left, right, mixed_mine = hold((far, theirs, left, sent[1], mixed_mine))

    right = lax.ppermute(right, "zh", SWAP)
    chunks = mine + far + theirs + [lax.ppermute(v, "c", SWAP) for v in far]
    d_inner, sums, cot = call_factor_grads(order, mixed_mine, tokens.T, chunks, room)
    sums = lax.all_to_all(sums.reshape(8, -1, block_out), DP, 0, 0)
    terms = call_quad_sum(kept, [left, right])
    delta = call_delta_rows(mixed, chunks)
    terms, sums, cot, delta = hold((terms, sums, cot, delta))

    parts = [turn(terms[d - 1], d) for d in (1, 2, 3)]
    sums = jnp.sum(sums.astype(F32), axis=0).astype(BF16)
    final = spread(sums, DP, 8)
    d_tokens = call_token_grads(base_weight, cot, factor, d_inner).T
    parts, d_tokens = hold((parts, d_tokens))

    output = terms[3] + delta
    for part in parts:
        output = output + part.astype(F32)
    d_first = final[:, :room].reshape(-1, block_out)[:hidden].astype(F32)
    d_second = final[:, room:].astype(F32)
    return (
        output,
        d_tokens,
        d_first.reshape(blocks, block_in, block_out),
        d_second.reshape(blocks, block_out, block_out),
    )


def solution(mesh):
    fine = Mesh(mesh.devices.reshape(2, 4, 2, 4, 2), ("zl", "x", "zh", "y", "c"))
    return jax.shard_map(
        per_device,
        mesh=fine,
        in_specs=(
            P(DP, TENSOR),
            P(TENSOR, None),
            P(TENSOR, None, None),
            P(TENSOR, None, None),
            P(),
            P(DP + TENSOR, None),
        ),
        out_specs=(
            P(DP + TENSOR, None),
            P(DP, TENSOR),
            P(TENSOR, None, None),
            P(TENSOR, None, None),
        ),
        check_vma=False,
    )
```

```python
import jax
import jax.numpy as jnp
from jax import lax
from jax.experimental import pallas as pl
from jax.experimental.pallas import tpu as pltpu
from jax.sharding import Mesh, PartitionSpec as P

F32 = jnp.float32
BF16 = jnp.bfloat16
DP = ("zl", "x")
TENSOR = ("zh", "y", "c")
SWAP = [(0, 1), (1, 0)]
TURNS = (1, 3, 2)
VMEM = pl.BlockSpec(memory_space=pltpu.VMEM)
ANY = pl.BlockSpec(memory_space=pl.ANY)
MIB = 1 << 20
CHUNKS = 10
HELD = ((0, 0, 0), (0, 1, 0), (1, 0, 1), (1, 1, 1), (2, 0, 3), (2, 1, 3), (3, 0, 2), (4, 0, 2))
SCALE = 100
KEPT = BF16
LEFT = 3
TILE = 2048


def params(mib):
    return pltpu.CompilerParams(vmem_limit_bytes=mib * MIB)


def cost(flops, moved):
    return pl.CostEstimate(flops=flops // SCALE, bytes_accessed=moved // SCALE, transcendentals=0)


def turn(value, by):
    return lax.ppermute(value, "y", [(i, (i + by) % 4) for i in range(4)])


def spread(value, axes, count):
    whole = jnp.broadcast_to(value[None], (count,) + value.shape)
    return lax.all_to_all(whole, axes, 0, 0)


def place_of():
    return lax.axis_index("c"), lax.axis_index("zh"), lax.axis_index("y")


def dot(a, b):
    return jnp.dot(a, b, preferred_element_type=F32)


def dot_nt(a, b):
    return lax.dot_general(a, b, (((1,), (1,)), ((), ())), preferred_element_type=F32)


def pack(cotangent, second, out):
    share, width = cotangent.shape
    block = second.shape[1]
    out[:, :width] = cotangent[...]
    for q in range(second.shape[0] // share):
        out[:, width + q * block : width + (q + 1) * block] = second[q * share : (q + 1) * share, :]


def call_pack(cotangent, second):
    share, width = cotangent.shape
    return pl.pallas_call(
        pack,
        in_specs=[VMEM] * 2,
        out_specs=VMEM,
        out_shape=jax.ShapeDtypeStruct((share, width + second.size // share), BF16),
        compiler_params=params(60),
        name="pack",
        cost_estimate=cost(share, share * width * 4),
    )(cotangent, second)


def base_rows(tokens, weight, other, own, held):
    step = pl.program_id(0)
    share = tokens.shape[0] // 16
    half = tokens.shape[0] // 2

    @pl.when(step == 0)
    def _():
        core, zh, y = place_of()
        for p in range(2):
            for z in range(2):
                for k in range(4):
                    c = 1 - core if p == 0 else core
                    zz = 1 - zh if z == 0 else zh
                    g = zz * 8 + lax.rem(y + (k + 1) % 4, 4) * 2 + c
                    at = p * half + (z * 4 + k) * share
                    held[at : at + share, :] = tokens[pl.ds(pl.multiple_of(g * share, share), share), :]

    total = dot(held[...], weight[...])
    other[...] = total[:half].astype(BF16)
    own[...] = total[half:].astype(own.dtype)


def call_base_rows(tokens, weight, tile=2048):
    rows, hidden = tokens.shape
    width = weight.shape[1]
    half = rows // 2
    return pl.pallas_call(
        base_rows,
        grid=(width // tile,),
        in_specs=[
            pl.BlockSpec((rows, hidden), lambda j: (0, 0)),
            pl.BlockSpec((hidden, tile), lambda j: (0, j)),
        ],
        out_specs=[pl.BlockSpec((half, tile), lambda j: (0, j))] * 2,
        out_shape=[
            jax.ShapeDtypeStruct((half, width), BF16),
            jax.ShapeDtypeStruct((half, width), KEPT),
        ],
        scratch_shapes=[pltpu.VMEM((rows, hidden), BF16)],
        compiler_params=params(60),
        name="base_rows",
        cost_estimate=cost(2 * rows * hidden * width, hidden * width * 2),
    )(tokens, weight)


def pair_sum(own, got, left, right, kept):
    total = own[...].astype(F32) + got[...].astype(F32)
    quarter = kept.shape[0]
    kept[...] = total[quarter:].astype(kept.dtype)
    step = pl.program_id(0)

    @pl.when(step < LEFT)
    def _():
        left[...] = total[:quarter].astype(BF16)

    @pl.when(step >= LEFT)
    def _():
        right[...] = total[:quarter].astype(BF16)


def call_pair_sum(own, got, tile=512):
    half, width = own.shape
    steps = width // tile
    out = (half // 2, tile)
    *sent, kept = pl.pallas_call(
        pair_sum,
        grid=(steps,),
        in_specs=[pl.BlockSpec((half, tile), lambda j: (0, j))] * 2,
        out_specs=[
            pl.BlockSpec(out, lambda j: (0, jnp.minimum(j, LEFT - 1))),
            pl.BlockSpec(out, lambda j: (0, jnp.maximum(j - LEFT, 0))),
            pl.BlockSpec(out, lambda j: (0, j)),
        ],
        out_shape=[
            jax.ShapeDtypeStruct((half // 2, LEFT * tile), BF16),
            jax.ShapeDtypeStruct((half // 2, width - LEFT * tile), BF16),
            jax.ShapeDtypeStruct((half // 2, width), KEPT),
        ],
        compiler_params=params(12),
        name="pair_sum",
        cost_estimate=cost(half * width, half * width * 6),
    )(own, got)
    return sent, kept


def quad_sum(kept, left, right, one, two, three, own):
    share = own.shape[0]
    cut = left.shape[1]
    for k, out in enumerate((one, two, three, own)):
        rows = slice(k * share, (k + 1) * share)
        out[:, :cut] = (kept[rows, :cut].astype(F32) + left[rows, :].astype(F32)).astype(out.dtype)
        out[:, cut:] = (kept[rows, cut:].astype(F32) + right[rows, :].astype(F32)).astype(out.dtype)


def call_quad_sum(kept, got):
    quarter, width = kept.shape
    share = quarter // 4
    return pl.pallas_call(
        quad_sum,
        in_specs=[VMEM] * 3,
        out_specs=[VMEM] * 4,
        out_shape=[jax.ShapeDtypeStruct((share, width), BF16)] * 3
        + [jax.ShapeDtypeStruct((share, width), F32)],
        compiler_params=params(60),
        name="quad_sum",
        cost_estimate=cost(quarter * width, quarter * width * 8),
    )(kept, *got)


def reorder(order, inner, out, flat):
    count, share, channels = inner.shape
    block = order.shape[1]
    per = channels // block
    tiles = count * per
    for t in range(tiles):
        flat[t] = inner[t // per, :, (t % per) * block : (t % per + 1) * block].astype(F32)

    def one(j):
        wanted = jnp.broadcast_to(order[pl.ds(j, 1), :], (share, block))
        lane = wanted % block
        tile = wanted // block
        total = jnp.zeros((share, block), F32)
        for t in range(tiles):
            found = jnp.take_along_axis(flat[t], lane, axis=1, mode="promise_in_bounds")
            total = jnp.where(tile == t, found, total)
        return total.astype(BF16)

    def group(g, _):
        for i in range(per):
            out[g, :, i * block : (i + 1) * block] = one(g * per + i)
        return 0

    lax.fori_loop(0, count, group, 0)


def call_reorder(order, inner):
    count, share, channels = inner.shape
    tiles, block = order.shape
    return pl.pallas_call(
        reorder,
        in_specs=[VMEM] * 2,
        out_specs=VMEM,
        out_shape=jax.ShapeDtypeStruct(inner.shape, BF16),
        scratch_shapes=[pltpu.VMEM((tiles, share, block), F32)],
        compiler_params=params(6),
        name="reorder",
        cost_estimate=cost(tiles * tiles * share * block * 4, count * share * channels * 4),
    )(order, inner)


def sources():
    core, zh, y = place_of()
    found = []
    for c in range(2):
        for slot, (chunk, row, back) in enumerate(HELD):
            cc = core if c == 0 else 1 - core
            zz = zh if slot % 2 == 0 else 1 - zh
            place = zz * 8 + lax.rem(y + 4 - back, 4) * 2 + cc
            found.append((c * 5 + chunk, row, place))
    return found


def block_of(ref, z, i, share, block, base=0):
    each = block // share
    parts = [
        ref[z * share : (z + 1) * share, base + (i * each + q) * block : base + (i * each + q + 1) * block]
        for q in range(each)
    ]
    return jnp.concatenate(parts, axis=0)


def delta_rows(mixed, *refs):
    chunks, out = refs[:CHUNKS], refs[CHUNKS]
    share = out.shape[0]
    block = mixed.shape[2] // 2
    for chunk, z, g in sources():
        for i in range(2):
            cols = pl.ds(pl.multiple_of((g * 2 + i) * block, block), block)
            factor = block_of(chunks[chunk], z, i, share, block)
            out[:, cols] = dot(mixed[g, :, i * block : (i + 1) * block], factor)


def call_delta_rows(mixed, chunks):
    groups, share, channels = mixed.shape
    width = groups * channels
    per = chunks[0].shape[1] - width
    second = [pl.BlockSpec((v.shape[0], per), lambda j: (0, width // per)) for v in chunks]
    return pl.pallas_call(
        delta_rows,
        grid=(1,),
        in_specs=[pl.BlockSpec(mixed.shape, lambda j: (0, 0, 0))] + second,
        out_specs=pl.BlockSpec((share, width), lambda j: (0, 0)),
        out_shape=jax.ShapeDtypeStruct((share, width), F32),
        compiler_params=params(60),
        name="delta_rows",
        cost_estimate=cost(share * width * channels, share * width * 6),
    )(mixed, *chunks)


def factor_grads(order, mixed, tokens_t, *refs):
    chunks, (d_inner, sums, cot_out, cot, routed, sem) = refs[:CHUNKS], refs[CHUNKS:]
    core, zh, y = place_of()
    block = order.shape[1]
    rows, channels = d_inner.shape
    share = rows // 16
    width = cot.shape[1]
    hidden = tokens_t.shape[0]
    found = sources()
    place = zh * 8 + y * 2 + core
    row = lax.broadcasted_iota(jnp.int32, (channels, block), 0) + place * channels
    for chunk, z, g in found:
        cot[pl.ds(pl.multiple_of(g * share, share), share), :] = chunks[chunk][
            z * share : (z + 1) * share, :width
        ]
        for i in range(2):
            n = g * 2 + i
            hits = jnp.where(row == order[pl.ds(n, 1), :], 1.0, 0.0).astype(BF16)
            factor = block_of(chunks[chunk], z, i, share, block, width)
            cols = pl.ds(pl.multiple_of(n * block, block), block)
            routed[:, cols] = dot(hits, factor).astype(BF16)
    copy = pltpu.make_async_copy(cot, cot_out, sem)
    copy.start()
    grad = dot_nt(cot[...], routed[...]).astype(BF16)
    d_inner[...] = grad
    whole = dot(tokens_t[...], grad)
    unit = lax.broadcasted_iota(jnp.int32, (hidden, block), 0)
    d_first = jnp.where(unit < hidden // 2, whole[:, :block], whole[:, block:]).astype(BF16)
    each = sums.shape[0] // 8
    few = channels // 8
    room = each - few
    for k in range(8):
        have = min(room, hidden - k * room)
        if have < room:
            sums[k * each : k * each + room, :] = jnp.zeros((room, block), BF16)
        sums[k * each : k * each + have, :] = d_first[k * room : k * room + have]
    mixed_t = mixed[...].reshape(rows, channels).T
    for i in range(channels // block):
        n = place * 2 + i
        cols = pl.ds(pl.multiple_of(n * block, block), block)
        d_second = dot(mixed_t[i * block : (i + 1) * block, :], cot[:, cols]).astype(BF16)
        for q in range(block // few):
            k = i * (block // few) + q
            sums[k * each + room : (k + 1) * each, :] = d_second[q * few : (q + 1) * few]
    copy.wait()


def call_factor_grads(order, mixed, tokens_t, chunks, room):
    groups, share, channels = mixed.shape
    rows = groups * share
    tiles, block = order.shape
    width = tiles * block
    each = room + channels // 8
    return pl.pallas_call(
        factor_grads,
        in_specs=[VMEM] * (3 + CHUNKS),
        out_specs=[VMEM, VMEM, ANY],
        out_shape=[
            jax.ShapeDtypeStruct((rows, channels), BF16),
            jax.ShapeDtypeStruct((8 * each, block), BF16),
            jax.ShapeDtypeStruct((rows, width), BF16),
        ],
        scratch_shapes=[
            pltpu.VMEM((rows, width), BF16),
            pltpu.VMEM((channels, width), BF16),
            pltpu.SemaphoreType.DMA,
        ],
        compiler_params=params(26),
        name="factor_grads",
        cost_estimate=cost(4 * rows * channels * width, rows * width * 2),
    )(order, mixed, tokens_t, *chunks)


def token_grads(weight, cot, factor, d_inner, out):
    term = dot_nt(weight[...], cot[...])

    @pl.when(pl.program_id(0) == 0)
    def _():
        hidden, block = factor.shape
        unit = lax.broadcasted_iota(jnp.int32, (hidden, block), 0)
        zero = jnp.zeros((hidden, block), BF16)
        first = jnp.where(unit < hidden // 2, factor[...], zero)
        second = jnp.where(unit < hidden // 2, zero, factor[...])
        wide = jnp.concatenate([first, second], axis=1)
        out[...] = term + dot_nt(wide, d_inner[...])

    @pl.when(pl.program_id(0) > 0)
    def _():
        out[...] += term


def call_token_grads(weight, cot, factor, d_inner, tile=TILE):
    hidden, width = weight.shape
    rows, channels = d_inner.shape
    return pl.pallas_call(
        token_grads,
        grid=(width // tile,),
        in_specs=[
            pl.BlockSpec((hidden, tile), lambda k: (0, k)),
            pl.BlockSpec((rows, tile), lambda k: (0, k)),
            pl.BlockSpec(factor.shape, lambda k: (0, 0)),
            pl.BlockSpec((rows, channels), lambda k: (0, 0)),
        ],
        out_specs=pl.BlockSpec((hidden, rows), lambda k: (0, 0)),
        out_shape=jax.ShapeDtypeStruct((hidden, rows), F32),
        compiler_params=params(60),
        name="token_grads",
        cost_estimate=cost(2 * rows * hidden * width, hidden * width * 2),
    )(weight, cot, factor, d_inner)


def per_device(tokens, base_weight, first_factor, second_factor, channel_order, cotangent):
    rows, hidden = tokens.shape
    blocks, block_in, block_out = first_factor.shape
    width = base_weight.shape[1]
    channels = blocks * block_out
    share = rows // 16
    room = -(-hidden // 128) * 16
    hold = lax.optimization_barrier
    order = channel_order.reshape(-1, block_out)

    bundle = call_pack(cotangent, second_factor.reshape(channels, block_out))
    partner = lax.ppermute(bundle, "zh", SWAP)
    factor = first_factor.reshape(hidden, block_out)
    block = jnp.arange(hidden, dtype=jnp.int32)[:, None] // block_in
    wide = jnp.concatenate([jnp.where(block == n, factor, 0) for n in range(blocks)], axis=1)
    inner = dot(tokens, wide).astype(BF16).reshape(16, share, channels)
    inner = lax.all_to_all(inner, TENSOR, 0, 0)
    other, own = call_base_rows(tokens, base_weight)
    bundle, partner, factor, inner, other, own = hold((bundle, partner, factor, inner, other, own))

    pair = jnp.concatenate([bundle, partner], axis=0)
    next_y, last_y = turn(pair, 1), turn(pair, 3)
    mixed = call_reorder(order, inner)
    sent, kept = call_pair_sum(own, lax.ppermute(other, "c", SWAP))
    theirs = [lax.ppermute(pair, "c", SWAP)]
    pair, next_y, last_y, mixed, sent, kept, theirs = hold(
        (pair, next_y, last_y, mixed, sent, kept, theirs)
    )

    far = [turn(next_y[:share], 1), turn(last_y[share:], 3)]
    mine = [pair, next_y, last_y]
    theirs = theirs + [lax.ppermute(v, "c", SWAP) for v in mine[1:]]
    mixed_mine = lax.all_to_all(mixed, TENSOR, 0, 0)
    left = lax.ppermute(sent[0], "zh", SWAP)
    far, theirs, left, right, mixed_mine = hold((far, theirs, left, sent[1], mixed_mine))

    right = lax.ppermute(right, "zh", SWAP)
    chunks = mine + far + theirs + [lax.ppermute(v, "c", SWAP) for v in far]
    d_inner, sums, cot = call_factor_grads(order, mixed_mine, tokens.T, chunks, room)
    sums = lax.all_to_all(sums.reshape(8, -1, block_out), DP, 0, 0)
    terms = call_quad_sum(kept, [left, right])
    delta = call_delta_rows(mixed, chunks)
    terms, sums, cot, delta = hold((terms, sums, cot, delta))

    parts = [turn(terms[d - 1], d) for d in (1, 2, 3)]
    sums = jnp.sum(sums.astype(F32), axis=0).astype(BF16)
    final = spread(sums, DP, 8)
    d_tokens = call_token_grads(base_weight, cot, factor, d_inner).T
    parts, d_tokens = hold((parts, d_tokens))

    output = terms[3] + delta
    for part in parts:
        output = output + part.astype(F32)
    d_first = final[:, :room].reshape(-1, block_out)[:hidden].astype(F32)
    d_second = final[:, room:].astype(F32)
    return (
        output,
        d_tokens,
        d_first.reshape(blocks, block_in, block_out),
        d_second.reshape(blocks, block_out, block_out),
    )


def solution(mesh):
    fine = Mesh(mesh.devices.reshape(2, 4, 2, 4, 2), ("zl", "x", "zh", "y", "c"))
    return jax.shard_map(
        per_device,
        mesh=fine,
        in_specs=(
            P(DP, TENSOR),
            P(TENSOR, None),
            P(TENSOR, None, None),
            P(TENSOR, None, None),
            P(),
            P(DP + TENSOR, None),
        ),
        out_specs=(
            P(DP + TENSOR, None),
            P(DP, TENSOR),
            P(TENSOR, None, None),
            P(TENSOR, None, None),
        ),
        check_vma=False,
    )
```
